128 devices in a mesh: gy: 16 (over y, x_hi, core), gx: 8 (over z, x_lo).
Axes of the slice: x: 4 (x_hi: 2, x_lo: 2; x = x_hi * 2 + x_lo), y: 4, z: 4, core: 2. Of those that a mesh axis runs over, the one named last changes fastest.
Arguments:
- level_set: float32 [256, 16384], P('gy', 'gx'), may hold values from -6 to 6
- spread_rate: float32 [256, 16384], P('gy', 'gx'), may hold values from 0.2 to 2
- cotangent: float32 [256, 16384], P('gy', 'gx'), may hold values from -6 to 6
Outputs:
- final_state: float32 [256, 16384], P('gy', 'gx')
- rate_gradient: float32 [256, 16384], P('gy', 'gx')
- initial_gradient: float32 [256, 16384], P('gy', 'gx')
The draws below stay inside these ranges and needn't reach their ends.
All inputs are finite; a program needn't handle non-finite values.
Results may differ from the reference program's by a relative error of at most 0.000029.
Values sent between devices are 32-bit elements; how exact they have to be, the bound alone decides.
No kernel may reach another device: no remote copies, remote signals or barrier semaphores. Data moves between devices by JAX's collectives and lax.ppermute only.
A program may use at most 128 MiB of HBM per device.

```python
import math
import jax
import jax.numpy as jnp

STEPS = 6
NY = 256
NX = 16384


def steps_of(key, dims, pieces, least, high):
    loudness, own = 1.0, jax.random.fold_in(key, 6)
    for dim, shards_of in pieces:
        steps = jnp.exp(jax.random.uniform(jax.random.fold_in(own, dim), (shards_of,), jnp.float32, least / len(pieces), high / len(pieces)))
        loudness = loudness * jnp.repeat(steps, dims[dim] // shards_of).reshape([-1 if axis == dim else 1 for axis in range(len(dims))])
    return loudness


def gaussian(rng, dims, spread, reach, shards=(), dtype=jnp.bfloat16):
    array = jax.random.normal(rng, dims, jnp.float32) * spread
    if len(shards) > 0:
        array = steps_of(rng, dims, shards, -0.22, 0.18) * array
    return jnp.clip(array, min=-reach, max=reach).astype(dtype)


def setup_inputs(seed: int = 0) -> dict:
    splits = jax.random.split(jax.random.key(seed), 4)
    level_set = gaussian(splits[0], (NY, NX), 1.0, 6.0, ((0, 16), (1, 8)), jnp.float32)
    spread_rate = jnp.clip(jnp.exp(math.log(2.0) - 2.3025851 * jax.random.uniform(splits[1], (NY, NX), jnp.float32) ** steps_of(splits[1], (NY, NX), ((0, 16), (1, 8)), -0.2, 0.2)), 0.2, 2.0)
    cotangent = gaussian(splits[2], (NY, NX), 1.0, 6.0, ((0, 16), (1, 8)), jnp.float32)
    return dict(level_set=level_set, spread_rate=spread_rate, cotangent=cotangent)


time_step = 0.2
smooth_eps = 0.001
speed_floor = 0.25

def weno(first, second, third, fourth, fifth):
    cand_one = first / 3.0 - 7.0 * second / 6.0 + 11.0 * third / 6.0
    cand_two = -second / 6.0 + 5.0 * third / 6.0 + fourth / 3.0
    cand_three = third / 3.0 + 5.0 * fourth / 6.0 - fifth / 6.0
    beta_one = 13.0 / 12.0 * (first - 2.0 * second + third) ** 2 + 0.25 * (first - 4.0 * second + 3.0 * third) ** 2
    beta_two = 13.0 / 12.0 * (second - 2.0 * third + fourth) ** 2 + 0.25 * (second - fourth) ** 2
    beta_three = 13.0 / 12.0 * (third - 2.0 * fourth + fifth) ** 2 + 0.25 * (3.0 * third - 4.0 * fourth + fifth) ** 2
    alpha_one = 0.1 / (smooth_eps + beta_one) ** 2
    alpha_two = 0.6 / (smooth_eps + beta_two) ** 2
    alpha_three = 0.3 / (smooth_eps + beta_three) ** 2
    return (alpha_one * cand_one + alpha_two * cand_two + alpha_three * cand_three) / (alpha_one + alpha_two + alpha_three)

def sides(diffs, count):
    left = weno(diffs[0:count], diffs[1:count + 1], diffs[2:count + 2], diffs[3:count + 3], diffs[4:count + 4])
    right = weno(diffs[5:count + 5], diffs[4:count + 4], diffs[3:count + 3], diffs[2:count + 2], diffs[1:count + 1])
    return (left, right)

def speed(padded):
    row_count = padded.shape[0] - 6
    col_count = padded.shape[1] - 6
    column_band = padded[:, 3:3 + col_count]
    left_y, right_y = sides(column_band[1:] - column_band[:-1], row_count)
    row_band = padded[3:3 + row_count, :]
    row_diffs = (row_band[:, 1:] - row_band[:, :-1]).T
    left_x, right_x = sides(row_diffs, col_count)
    left_x, right_x = (left_x.T, right_x.T)
    square = jnp.maximum(left_y, 0.0) ** 2 + jnp.minimum(right_y, 0.0) ** 2
    square = square + jnp.maximum(left_x, 0.0) ** 2 + jnp.minimum(right_x, 0.0) ** 2
    return jnp.sqrt(square + speed_floor)

def periodic(state):
    return jnp.pad(state, 3, mode='wrap')

def reference(level_set, spread_rate, cotangent):
    stored = []
    state = level_set
    for step in range(STEPS):
        stored.append(state)
        middle = state - time_step * spread_rate * speed(periodic(state))
        stored.append(middle)
        state = 0.5 * state + 0.5 * (middle - time_step * spread_rate * speed(periodic(middle)))
    final_state = state

    def adjoint(source, weight):
        value, pull_back = jax.vjp(speed, periodic(source))
        grad_pad, = pull_back(spread_rate * weight)
        back = grad_pad[3:-3, 3:-3]
        back = back.at[-3:, :].add(grad_pad[0:3, 3:-3])
        back = back.at[0:3, :].add(grad_pad[-3:, 3:-3])
        back = back.at[:, -3:].add(grad_pad[3:-3, 0:3])
        back = back.at[:, 0:3].add(grad_pad[3:-3, -3:])
        return (back, value)
    adjoint_state = cotangent
    rate_gradient = jnp.zeros_like(spread_rate)
    for step in reversed(range(STEPS)):
        weight_late = 0.5 * time_step * adjoint_state
        back_late, value_late = adjoint(stored[2 * step + 1], weight_late)
        adjoint_middle = 0.5 * adjoint_state - back_late
        rate_gradient = rate_gradient - weight_late * value_late
        weight_early = time_step * adjoint_middle
        back_early, value_early = adjoint(stored[2 * step], weight_early)
        rate_gradient = rate_gradient - weight_early * value_early
        adjoint_state = 0.5 * adjoint_state + adjoint_middle - back_early
    return (final_state, rate_gradient, adjoint_state)
```

```python
import functools

import jax
import jax.numpy as jnp
from jax import lax
from jax.experimental import pallas as pl
from jax.experimental.pallas import tpu as pltpu
from jax.sharding import PartitionSpec as P

STEPS = 6
STAGES = 2 * STEPS
DT = 0.2
EPS = 0.001
FLOOR = 0.25

WIDTH = 128
HALO = 72
HALO_COT = 40
PAD = 16
BLOCK = 16
TILES = (WIDTH + 2 * HALO) // 8
OWN = PAD + HALO
IDLE = PAD + 2 * HALO + WIDTH + 16
ROWS = IDLE + BLOCK + 8
PARITIES = (0, 1)


def shift_lanes(value, by):
    return pltpu.roll(value, by % 128, 1)


def window_of(even, odd):
    return (
        shift_lanes(odd, 2),
        shift_lanes(even, 1),
        shift_lanes(odd, 1),
        shift_lanes(even, -1),
        shift_lanes(odd, -1),
    )


def third_differences(window):
    m = [b - a for a, b in zip(window[:-1], window[1:])]
    d = [b - a for a, b in zip(m[:-1], m[1:])]
    e = [b - a for a, b in zip(d[:-1], d[1:])]
    t = [0.5 * (a + b) for a, b in zip(d[:-1], d[1:])]
    return m, e, t


def smoothness(e, t):
    h = EPS + (13.0 / 12.0 * e) * e
    return (
        lambda: h + (t + e) * (t + e),
        lambda: h + t * t,
        lambda: h + (t - e) * (t - e),
    )


def ratios(i1, g2, i3):
    x = g2 * i1
    y = g2 * i3
    return x * x, y * y


def left_value(base, x, y, f1, f2):
    a, b = x * f1, y * f2
    s = a + b
    denominator = (x + 6.0) + 3.0 * y
    return base + ((s + s) + b) * (1.0 / denominator)


def right_value(base, x, y, f1, f2):
    a, b = x * f1, y * f2
    s = a + b
    denominator = (y + 6.0) + 3.0 * x
    return base - ((s + s) + a) * (1.0 / denominator)


def left_base(m0, m1, m2):
    return (5.0 / 6.0) * m1 + ((1.0 / 3.0) * m2 - (1.0 / 6.0) * m0)


def right_base(m0, m1, m2):
    return (5.0 / 6.0) * m1 + ((1.0 / 3.0) * m0 - (1.0 / 6.0) * m2)


def face_adjoint(aL, aR, i1, g2, i3, f1, f2):
    x, y = ratios(i1, g2, i3)
    a, b = x * f1, y * f2
    s2 = a + b
    s2 = s2 + s2
    s6 = (x + y) + 6.0
    kL = 1.0 / (s6 + (y + y))
    kR = 1.0 / (s6 + (x + x))
    bL = aL * kL
    bR = -(aR * kR)
    cL = bL * ((s2 + b) * kL)
    cR = bR * ((s2 + a) * kR)
    bs = bL + bR
    bs = bs + bs
    on_a = bs + bR
    on_b = bs + bL
    cs = cL + cR
    gf1 = x * on_a
    gf2 = y * on_b
    gX = f1 * gf1 - x * (cs + (cR + cR))
    gY = f2 * gf2 - y * (cs + (cL + cL))
    i2 = 1.0 / g2
    return (
        -(gX * i1),
        (gX + gY) * i2,
        -(gY * i3),
        (1.0 / 6.0) * gf1,
        (1.0 / 6.0) * gf2,
        (1.0 / 6.0) * aL - (1.0 / 3.0) * aR,
        (1.0 / 3.0) * aL - (1.0 / 6.0) * aR,
        aL + aR,
    )


def forward_start(s):
    return PAD + 8 * ((3 * (s + 1)) // 8) - 8


def forward_end(s):
    return PAD + 8 * (TILES - (3 * (s + 1)) // 8) + 8


def backward_start(s):
    return PAD + 8 * ((39 + 3 * (STAGES - 1 - s)) // 8) - 8


def backward_end(s):
    return PAD + 8 * (TILES - (39 + 3 * (STAGES - 1 - s)) // 8) + 8


def kernel(core, from_left, from_right, out, U, i1x, g2x, i3x, mLx, mRx, i1y, g2y, i3y, mLy, mRy, rinv, dtr, g, held, rga, win, e6, tx, aux, fx, fy, ey, RT, stage_out):
    own = slice(OWN, OWN + WIDTH)
    low = slice(PAD, PAD + HALO)
    high = slice(OWN + WIDTH, OWN + WIDTH + HALO)
    held[...] = jnp.zeros_like(held)
    rga[...] = jnp.zeros_like(rga)
    for p in PARITIES:
        U[0, p, own, :] = core[0, p]
        U[0, p, low, :] = from_left[p, 0:HALO, :]
        U[0, p, high, :] = from_right[p, 0:HALO, :]
        dtr[p, own, :] = DT * core[1, p]
        dtr[p, low, :] = DT * from_left[p, HALO : 2 * HALO, :]
        dtr[p, high, :] = DT * from_right[p, HALO : 2 * HALO, :]
        g[p, own, :] = 0.5 * core[2, p]
        g[p, OWN - HALO_COT : OWN, :] = 0.5 * from_left[p, 2 * HALO :, :]
        g[p, OWN + WIDTH : OWN + WIDTH + HALO_COT, :] = 0.5 * from_right[p, 2 * HALO :, :]

    def rows(r, offset=0):
        return pl.ds(r + offset, BLOCK)

    def aligned(r):
        return pl.multiple_of(r, 8)

    def columns_of(s, r):
        for p in PARITIES:
            um, u0, u1, u2 = (U[s, p, rows(r, o), :] for o in (-1, 0, 1, 2))
            m0, m1, m2 = u0 - um, u1 - u0, u2 - u1
            d0, d1 = m1 - m0, m2 - m1
            e = d1 - d0
            t = 0.5 * (d0 + d1)
            s1, s2, s3 = smoothness(e, t)
            i1x[s, p, rows(r), :] = 1.0 / s1()
            g2x[s, p, rows(r), :] = s2()
            i3x[s, p, rows(r), :] = 1.0 / s3()
            e6[p, rows(r), :] = (1.0 / 6.0) * e

    def windows(s, r):
        for n, value in enumerate(window_of(U[s, 0, rows(r), :], U[s, 1, rows(r), :])):
            win[n, rows(r), :] = value

    def load_window(s, r):
        return [
            win[0, rows(r), :],
            win[1, rows(r), :],
            win[2, rows(r), :],
            U[s, 0, rows(r), :],
            U[s, 1, rows(r), :],
            win[3, rows(r), :],
            win[4, rows(r), :],
        ]

    def faces(s, r):
        squares = []
        for p in PARITIES:
            u = [U[s, p, rows(r, o), :] for o in (-2, -1, 0, 1, 2)]
            m = [b - a for a, b in zip(u[:-1], u[1:])]
            e = [e6[p, rows(r, o), :] for o in (-2, -1, 0, 1)]
            f = [a - b for a, b in zip(e[:-1], e[1:])]
            x, y = ratios(i1x[s, p, rows(r, -2), :], g2x[s, p, rows(r, -1), :], i3x[s, p, rows(r), :])
            left = jnp.maximum(left_value(left_base(m[0], m[1], m[2]), x, y, f[0], f[1]), 0.0)
            x, y = ratios(i1x[s, p, rows(r, -1), :], g2x[s, p, rows(r), :], i3x[s, p, rows(r, 1), :])
            right = jnp.minimum(right_value(right_base(m[1], m[2], m[3]), x, y, f[1], f[2]), 0.0)
            mLx[s, p, rows(r), :] = left
            mRx[s, p, rows(r), :] = right
            squares.append(left * left + right * right)
        window = load_window(s, r)
        m, e, t = third_differences(window)
        terms = [smoothness(a, b) for a, b in zip(e, t)]
        for p in PARITIES:
            i1 = 1.0 / terms[p][0]()
            g2 = terms[p + 1][1]()
            i3 = 1.0 / terms[p + 2][2]()
            i1y[s, p, rows(r), :] = i1
            g2y[s, p, rows(r), :] = g2
            i3y[s, p, rows(r), :] = i3
            x, y = ratios(i1, g2, i3)
            f1 = (1.0 / 6.0) * (e[p] - e[p + 1])
            f2 = (1.0 / 6.0) * (e[p + 1] - e[p + 2])
            a, b = x * f1, y * f2
            s2 = a + b
            s2 = s2 + s2
            s6 = (x + y) + 6.0
            ms = (m[p + 1], m[p + 2], m[p + 3])
            left = left_base(*ms) + (s2 + b) * (1.0 / (s6 + (y + y)))
            right = right_base(*ms) - (s2 + a) * (1.0 / (s6 + (x + x)))
            left = jnp.maximum(left, 0.0)
            right = jnp.minimum(right, 0.0)
            mLy[s, p, rows(r), :] = left
            mRy[s, p, rows(r), :] = right
            squares[p] = squares[p] + left * left
            if p == 1:
                squares[0] = squares[0] + right * right
        for p in PARITIES:
            aux[p, rows(r), :] = squares[p] + FLOOR

    def advance(s, r):
        late = (s % 2).astype(jnp.float32)
        keep = 0.5 * late
        take = 1.0 - keep
        before = jnp.maximum(s - 1, 0)
        for p in PARITIES:
            square = aux[p, rows(r), :]
            if p == 1:
                right = shift_lanes(mRy[s, 0, rows(r), :], -1)
                square = square + right * right
            inverse = lax.rsqrt(square)
            rinv[s, p, rows(r), :] = inverse
            moved = U[s, p, rows(r), :] - dtr[p, rows(r), :] * (square * inverse)
            U[s + 1, p, rows(r), :] = keep * U[before, p, rows(r), :] + take * moved

    def forward_next(s, r):
        over = r + BLOCK >= forward_end(s)
        last = jnp.logical_and(over, s == STAGES - 1)
        done = r == IDLE
        s_next = jnp.where(over, jnp.minimum(s + 1, STAGES - 1), s)
        r_next = jnp.where(over, forward_start(s_next), r + BLOCK)
        r_next = jnp.where(jnp.logical_or(last, done), IDLE, r_next)
        return s_next, r_next

    forward_count = sum(-(-(forward_end(s) - forward_start(s)) // BLOCK) for s in range(STAGES))

    def forward_step(_, state):
        (s0, r0), (s1, r1), (s2, r2), (s3, r3) = state
        advance(s3, aligned(r3))
        faces(s2, aligned(r2))
        windows(s0, aligned(r0))
        columns_of(s0, aligned(r0))
        return (forward_next(s0, r0), (s0, r0), (s1, r1), (s2, r2))

    zero = jnp.int32(0)
    idle = jnp.int32(IDLE)
    lax.fori_loop(
        0,
        forward_count + 3,
        forward_step,
        ((zero, jnp.int32(forward_start(0))), (zero, idle), (zero, idle), (zero, idle)),
    )

    def weigh(s, r):
        for p in PARITIES:
            weight = g[p, rows(r), :]
            inverse = rinv[s, p, rows(r), :]
            rga[p, rows(r), :] = rga[p, rows(r), :] + weight * (1.0 / inverse)
            w = (dtr[p, rows(r), :] * weight) * inverse
            aux[p, rows(r), :] = w
            if p == 1:
                aux[2, rows(r), :] = shift_lanes(w, 1)
            um, u0, u1, u2 = (U[s, p, rows(r, o), :] for o in (-1, 0, 1, 2))
            m0, m1, m2 = u0 - um, u1 - u0, u2 - u1
            d0, d1 = m1 - m0, m2 - m1
            e6[p, rows(r), :] = (1.0 / 6.0) * (d1 - d0)
            tx[p, rows(r), :] = 0.5 * (d0 + d1)
        windows(s, r)

    def face_adjoints(s, r):
        for p in PARITIES:
            aL = aux[p, rows(r), :] * mLx[s, p, rows(r), :]
            aR = aux[p, rows(r, -1), :] * mRx[s, p, rows(r, -1), :]
            e = [e6[p, rows(r, o), :] for o in (-2, -1, 0)]
            parts = face_adjoint(
                aL, aR,
                i1x[s, p, rows(r, -2), :], g2x[s, p, rows(r, -1), :], i3x[s, p, rows(r), :],
                e[0] - e[1], e[1] - e[2],
            )
            for n, part in enumerate(parts):
                fx[n, p, rows(r), :] = part
        _, e, t = third_differences(load_window(s, r))
        for n in range(4):
            ey[n, rows(r), :] = e[n]
            ey[n + 4, rows(r), :] = t[n]
        for p in PARITIES:
            aL = aux[p, rows(r), :] * mLy[s, p, rows(r), :]
            aR = aux[0 if p == 1 else 2, rows(r), :] * mRy[s, p, rows(r), :]
            parts = face_adjoint(
                aL, aR,
                i1y[s, p, rows(r), :], g2y[s, p, rows(r), :], i3y[s, p, rows(r), :],
                (1.0 / 6.0) * (e[p] - e[p + 1]), (1.0 / 6.0) * (e[p + 1] - e[p + 2]),
            )
            for n, part in enumerate(parts):
                fy[n, p, rows(r), :] = part

    def rows_adjoint(s, r):
        e = [ey[n, rows(r), :] for n in range(4)]
        t = [ey[n + 4, rows(r), :] for n in range(4)]
        (g1e, g2e, g3e, f1e, f2e, bqe, bre, ame), (g1o, g2o, g3o, f1o, f2o, bqo, bro, amo) = (
            [fy[n, p, rows(r), :] for n in range(8)] for p in PARITIES
        )
        v0 = 4.0 * ((t[0] + e[0]) * g1e)
        v1o = 4.0 * ((t[1] + e[1]) * g1o)
        v1e = 4.0 * (t[1] * g2e)
        v2e = 4.0 * ((t[2] - e[2]) * g3e)
        v2o = 4.0 * (t[2] * g2o)
        v3 = 4.0 * ((t[3] - e[3]) * g3o)
        c = 13.0 / 3.0
        on_e = [
            (c * e[0]) * g1e + v0 + f1e,
            (c * e[1]) * (g2e + g1o) + v1o + ((f2e - f1e) + f1o),
            (c * e[2]) * (g3e + g2o) - v2e + ((f2o - f1o) - f2e),
            (c * e[3]) * g3o - v3 - f2o,
        ]
        on_t = [0.5 * v0, 0.5 * (v1e + v1o), 0.5 * (v2e + v2o), 0.5 * v3]
        lower = [b - a for a, b in zip(on_e, on_t)]
        upper = [b + a for a, b in zip(on_e, on_t)]
        d = [
            lower[0],
            lower[1] + upper[0] + bqe,
            lower[2] + upper[1] + (bre + bqo),
            lower[3] + upper[2] + bro,
            upper[3],
        ]
        m = [d[0] - d[1], (d[1] - d[2]) + ame, (d[2] - d[3]) + amo, d[3] - d[4]]
        u = [d[0], -d[0] - m[0], m[0] - m[1], m[1] - m[2], m[2] - m[3], m[3] - d[4], d[4]]
        RT[4, rows(r), :] = u[3] + (shift_lanes(u[1], -1) + shift_lanes(u[5], 1))
        RT[5, rows(r), :] = u[4] + (shift_lanes(u[0], -2) + shift_lanes(u[2], -1)) + shift_lanes(u[6], 1)

    def columns_adjoint(s, r):
        for p in PARITIES:
            e = 6.0 * e6[p, rows(r), :]
            t = tx[p, rows(r), :]
            g1 = fx[0, p, rows(r, 2), :]
            g2 = fx[1, p, rows(r, 1), :]
            g3 = fx[2, p, rows(r), :]
            v1 = (t + e) * g1
            v2 = t * g2
            v3 = (t - e) * g3
            fs = (fx[3, p, rows(r, 2), :] - fx[3, p, rows(r, 1), :]) + (fx[4, p, rows(r, 1), :] - fx[4, p, rows(r), :])
            on_e = ((13.0 / 3.0) * e) * ((g1 + g2) + g3) + 4.0 * (v1 - v3) + fs
            on_t = 2.0 * ((v1 + v2) + v3)
            RT[p, rows(r), :] = (on_t - on_e) + fx[6, p, rows(r), :]
            RT[p + 2, rows(r), :] = (on_t + on_e) + fx[5, p, rows(r, 2), :]

    def retreat(s, r):
        early = (1 - s % 2).astype(jnp.float32)
        scale = 1.0 - 0.5 * early
        for p in PARITIES:
            d = [RT[p, rows(r, o), :] + RT[p + 2, rows(r, o - 1), :] for o in (-1, 0, 1)]
            back = (fx[7, p, rows(r), :] - fx[7, p, rows(r, 1), :]) + ((d[0] - d[1]) + (d[2] - d[1]))
            back = back + RT[4 + p, rows(r), :]
            old = g[p, rows(r), :]
            g[p, rows(r), :] = scale * ((old - back) + early * held[p, rows(r), :])
            held[p, rows(r), :] = old

    def backward_next(s, r):
        over = r + BLOCK >= backward_end(s)
        last = jnp.logical_and(over, s == 0)
        done = r == IDLE
        s_next = jnp.where(over, jnp.maximum(s - 1, 0), s)
        r_next = jnp.where(over, backward_start(s_next), r + BLOCK)
        r_next = jnp.where(jnp.logical_or(last, done), IDLE, r_next)
        return s_next, r_next

    backward_count = sum(-(-(backward_end(s) - backward_start(s)) // BLOCK) for s in range(STAGES))

    def backward_step(_, state):
        retreat(state[5][0], aligned(state[5][1]))
        columns_adjoint(state[3][0], aligned(state[3][1]))
        rows_adjoint(state[2][0], aligned(state[2][1]))
        face_adjoints(state[1][0], aligned(state[1][1]))
        weigh(state[0][0], aligned(state[0][1]))
        return (backward_next(*state[0]),) + state[:5]

    last = jnp.int32(STAGES - 1)
    lax.fori_loop(
        0,
        backward_count + 5,
        backward_step,
        ((last, jnp.int32(backward_start(STAGES - 1))),) + ((last, idle),) * 5,
    )

    for n in range(3):
        for p in PARITIES:
            if n == 0:
                value = U[STAGES, p, own, :]
            elif n == 1:
                value = -DT * rga[p, own, :]
            else:
                value = 2.0 * g[p, own, :]
            stage_out[pl.ds(p, 128, stride=2), :] = value.T
        for device in range(16):
            out[device, n] = stage_out[16 * device : 16 * device + 16, :]


def sweep(core, from_left, from_right):
    full = (2, ROWS, 128)
    f32 = jnp.float32
    staged = pltpu.VMEM((STAGES,) + full, f32)
    plain = pltpu.VMEM(full, f32)
    return pl.pallas_call(
        kernel,
        out_shape=jax.ShapeDtypeStruct((16, 3, 16, 128), f32),
        in_specs=[pl.BlockSpec(memory_space=pltpu.VMEM)] * 3,
        out_specs=pl.BlockSpec(memory_space=pltpu.VMEM),
        scratch_shapes=[pltpu.VMEM((STAGES + 1,) + full, f32)]
        + [staged] * 11
        + [
            plain,
            plain,
            plain,
            plain,
            pltpu.VMEM((5, ROWS, 128), f32),
            plain,
            plain,
            pltpu.VMEM((3, ROWS, 128), f32),
            pltpu.VMEM((8,) + full, f32),
            pltpu.VMEM((8,) + full, f32),
            pltpu.VMEM((8, ROWS, 128), f32),
            pltpu.VMEM((6, ROWS, 128), f32),
            pltpu.VMEM((256, 128), f32),
        ],
        compiler_params=pltpu.CompilerParams(vmem_limit_bytes=63 * 2**20),
    )(core, from_left, from_right)


def turn_kernel(blocks, core, low, high, rows_ref):
    for n in range(3):
        for device in range(16):
            rows_ref[16 * device : 16 * device + 16, :] = blocks[device, n]
        for p in PARITIES:
            core[n, p] = rows_ref[pl.ds(p, 128, stride=2), :].T
    for p in PARITIES:
        for n, (width, start) in enumerate(((HALO, 0), (HALO, HALO), (HALO_COT, 2 * HALO))):
            low[p, start : start + width, :] = core[n, p, 0:width, :]
            high[p, start : start + width, :] = core[n, p, WIDTH - width : WIDTH, :]


def turn(blocks):
    f32 = jnp.float32
    edge = jax.ShapeDtypeStruct((2, 2 * HALO + HALO_COT, 128), f32)
    return pl.pallas_call(
        turn_kernel,
        out_shape=(jax.ShapeDtypeStruct((3, 2, 128, 128), f32), edge, edge),
        in_specs=[pl.BlockSpec(memory_space=pltpu.VMEM)],
        out_specs=[pl.BlockSpec(memory_space=pltpu.VMEM)] * 3,
        scratch_shapes=[pltpu.VMEM((256, 128), f32)],
    )(blocks)


def shards(level_set, spread_rate, cotangent):
    bands, runs = lax.axis_size("gy"), lax.axis_size("gx")
    stacked = jnp.stack([level_set, spread_rate, cotangent])
    blocks = stacked.reshape(3, 16, bands, WIDTH).transpose(2, 0, 1, 3)
    blocks = lax.all_to_all(blocks, "gy", 0, 0)
    core, low, high = turn(blocks)
    order = [(k, x) for x in range(runs) for k in range(bands)]
    place = [k * runs + x for k, x in order]
    up = list(zip(place, place[1:] + place[:1]))
    from_left = lax.ppermute(high, ("gy", "gx"), up)
    from_right = lax.ppermute(low, ("gy", "gx"), [(b, a) for a, b in up])
    done = lax.all_to_all(sweep(core, from_left, from_right), "gy", 0, 0)
    done = done.transpose(1, 2, 0, 3).reshape(3, 16, bands * WIDTH)
    return (done[0], done[1], done[2])


def solution(mesh):
    spec = P("gy", "gx")
    return jax.shard_map(
        shards, mesh=mesh, in_specs=(spec,) * 3, out_specs=(spec,) * 3, check_vma=False
    )
```

```python
import functools

import jax
import jax.numpy as jnp
from jax import lax
from jax.experimental import pallas as pl
from jax.experimental.pallas import tpu as pltpu
from jax.sharding import PartitionSpec as P

STEPS = 6
STAGES = 2 * STEPS
DT = 0.2
EPS = 0.001
FLOOR = 0.25

WIDTH = 128
HALO = 72
HALO_COT = 40
PAD = 16
BLOCK = 16
TILES = (WIDTH + 2 * HALO) // 8
OWN = PAD + HALO
IDLE = PAD + 2 * HALO + WIDTH + 16
ROWS = IDLE + BLOCK + 8
PARITIES = (0, 1)


def shift_lanes(value, by):
    return pltpu.roll(value, by % 128, 1)


def window_of(even, odd):
    return (
        shift_lanes(odd, 2),
        shift_lanes(even, 1),
        shift_lanes(odd, 1),
        shift_lanes(even, -1),
        shift_lanes(odd, -1),
    )


def third_differences(window):
    m = [b - a for a, b in zip(window[:-1], window[1:])]
    d = [b - a for a, b in zip(m[:-1], m[1:])]
    e = [b - a for a, b in zip(d[:-1], d[1:])]
    t = [0.5 * (a + b) for a, b in zip(d[:-1], d[1:])]
    return m, e, t


def smoothness(e, t):
    h = EPS + (13.0 / 12.0 * e) * e
    return (
        lambda: h + (t + e) * (t + e),
        lambda: h + t * t,
        lambda: h + (t - e) * (t - e),
    )


def ratios(i1, g2, i3):
    x = g2 * i1
    y = g2 * i3
    return x * x, y * y


def left_value(base, x, y, f1, f2):
    a, b = x * f1, y * f2
    s = a + b
    denominator = (x + 6.0) + 3.0 * y
    return base + ((s + s) + b) * (1.0 / denominator)


def right_value(base, x, y, f1, f2):
    a, b = x * f1, y * f2
    s = a + b
    denominator = (y + 6.0) + 3.0 * x
    return base - ((s + s) + a) * (1.0 / denominator)


def left_base(m0, m1, m2):
    return (5.0 / 6.0) * m1 + ((1.0 / 3.0) * m2 - (1.0 / 6.0) * m0)


def right_base(m0, m1, m2):
    return (5.0 / 6.0) * m1 + ((1.0 / 3.0) * m0 - (1.0 / 6.0) * m2)


def face_adjoint(aL, aR, i1, g2, i3, f1, f2):
    x, y = ratios(i1, g2, i3)
    a, b = x * f1, y * f2
    s2 = a + b
    s2 = s2 + s2
    s6 = (x + y) + 6.0
    kL = 1.0 / (s6 + (y + y))
    kR = 1.0 / (s6 + (x + x))
    bL = aL * kL
    bR = -(aR * kR)
    cL = bL * ((s2 + b) * kL)
    cR = bR * ((s2 + a) * kR)
    bs = bL + bR
    bs = bs + bs
    on_a = bs + bR
    on_b = bs + bL
    cs = cL + cR
    gf1 = x * on_a
    gf2 = y * on_b
    gX = f1 * gf1 - x * (cs + (cR + cR))
    gY = f2 * gf2 - y * (cs + (cL + cL))
    i2 = 1.0 / g2
    return (
        -(gX * i1),
        (gX + gY) * i2,
        -(gY * i3),
        (1.0 / 6.0) * gf1,
        (1.0 / 6.0) * gf2,
        (1.0 / 6.0) * aL - (1.0 / 3.0) * aR,
        (1.0 / 3.0) * aL - (1.0 / 6.0) * aR,
        aL + aR,
    )


def forward_start(s):
    return PAD + 8 * ((3 * (s + 1)) // 8) - 8


def forward_end(s):
    return PAD + 8 * (TILES - (3 * (s + 1)) // 8) + 8


def backward_start(s):
    return PAD + 8 * ((39 + 3 * (STAGES - 1 - s)) // 8) - 8


def backward_end(s):
    return PAD + 8 * (TILES - (39 + 3 * (STAGES - 1 - s)) // 8) + 8


def kernel(core, from_left, from_right, out, U, i1x, g2x, i3x, mLx, mRx, i1y, g2y, i3y, mLy, mRy, rinv, dtr, g, held, rga, win, e6, tx, aux, fx, fy, ey, RT, stage_out):
    own = slice(OWN, OWN + WIDTH)
    low = slice(PAD, PAD + HALO)
    high = slice(OWN + WIDTH, OWN + WIDTH + HALO)
    held[...] = jnp.zeros_like(held)
    rga[...] = jnp.zeros_like(rga)
    for p in PARITIES:
        U[0, p, own, :] = core[0, p]
        U[0, p, low, :] = from_left[p, 0:HALO, :]
        U[0, p, high, :] = from_right[p, 0:HALO, :]
        dtr[p, own, :] = DT * core[1, p]
        dtr[p, low, :] = DT * from_left[p, HALO : 2 * HALO, :]
        dtr[p, high, :] = DT * from_right[p, HALO : 2 * HALO, :]
        g[p, own, :] = 0.5 * core[2, p]
        g[p, OWN - HALO_COT : OWN, :] = 0.5 * from_left[p, 2 * HALO :, :]
        g[p, OWN + WIDTH : OWN + WIDTH + HALO_COT, :] = 0.5 * from_right[p, 2 * HALO :, :]

    def rows(r, offset=0):
        return pl.ds(r + offset, BLOCK)

    def aligned(r):
        return pl.multiple_of(r, 8)

    def together(*phases):
        for phase in phases:
            next(phase)
        stores = [store for phase in phases for store in next(phase)]
        for ref, index, value in stores:
            ref[index] = value

    def columns_of(s, r):
        us = [[U[s, p, rows(r, o), :] for o in (-1, 0, 1, 2)] for p in PARITIES]
        yield
        stores = []
        for p in PARITIES:
            um, u0, u1, u2 = us[p]
            m0, m1, m2 = u0 - um, u1 - u0, u2 - u1
            d0, d1 = m1 - m0, m2 - m1
            e = d1 - d0
            t = 0.5 * (d0 + d1)
            s1, s2, s3 = smoothness(e, t)
            at = (s, p, rows(r), slice(None))
            stores += [
                (i1x, at, 1.0 / s1()),
                (g2x, at, s2()),
                (i3x, at, 1.0 / s3()),
                (e6, at[1:], (1.0 / 6.0) * e),
            ]
        stores += [
            (win, (n, rows(r), slice(None)), value) for n, value in enumerate(window_of(us[0][1], us[1][1]))
        ]
        yield stores

    def load_window(s, r):
        return [
            win[0, rows(r), :],
            win[1, rows(r), :],
            win[2, rows(r), :],
            U[s, 0, rows(r), :],
            U[s, 1, rows(r), :],
            win[3, rows(r), :],
            win[4, rows(r), :],
        ]

    def faces(s, r):
        loads = []
        for p in PARITIES:
            loads.append((
                [U[s, p, rows(r, o), :] for o in (-2, -1, 0, 1, 2)],
                [e6[p, rows(r, o), :] for o in (-2, -1, 0, 1)],
                [i1x[s, p, rows(r, o), :] for o in (-2, -1)],
                [g2x[s, p, rows(r, o), :] for o in (-1, 0)],
                [i3x[s, p, rows(r, o), :] for o in (0, 1)],
            ))
        window = load_window(s, r)
        yield
        squares, stores = [], []
        for p in PARITIES:
            u, e, i1, g2, i3 = loads[p]
            m = [b - a for a, b in zip(u[:-1], u[1:])]
            f = [a - b for a, b in zip(e[:-1], e[1:])]
            x, y = ratios(i1[0], g2[0], i3[0])
            left = jnp.maximum(left_value(left_base(m[0], m[1], m[2]), x, y, f[0], f[1]), 0.0)
            x, y = ratios(i1[1], g2[1], i3[1])
            right = jnp.minimum(right_value(right_base(m[1], m[2], m[3]), x, y, f[1], f[2]), 0.0)
            at = (s, p, rows(r), slice(None))
            stores += [(mLx, at, left), (mRx, at, right)]
            squares.append(left * left + right * right)
        m, e, t = third_differences(window)
        terms = [smoothness(a, b) for a, b in zip(e, t)]
        for p in PARITIES:
            i1 = 1.0 / terms[p][0]()
            g2 = terms[p + 1][1]()
            i3 = 1.0 / terms[p + 2][2]()
            x, y = ratios(i1, g2, i3)
            f1 = (1.0 / 6.0) * (e[p] - e[p + 1])
            f2 = (1.0 / 6.0) * (e[p + 1] - e[p + 2])
            a, b = x * f1, y * f2
            s2 = a + b
            s2 = s2 + s2
            s6 = (x + y) + 6.0
            ms = (m[p + 1], m[p + 2], m[p + 3])
            left = left_base(*ms) + (s2 + b) * (1.0 / (s6 + (y + y)))
            right = right_base(*ms) - (s2 + a) * (1.0 / (s6 + (x + x)))
            left = jnp.maximum(left, 0.0)
            right = jnp.minimum(right, 0.0)
            at = (s, p, rows(r), slice(None))
            stores += [(i1y, at, i1), (g2y, at, g2), (i3y, at, i3), (mLy, at, left), (mRy, at, right)]
            squares[p] = squares[p] + left * left
            if p == 1:
                squares[0] = squares[0] + right * right
        for p in PARITIES:
            stores.append((aux, (p, rows(r), slice(None)), squares[p] + FLOOR))
        yield stores

    def advance(s, r):
        late = (s % 2).astype(jnp.float32)
        keep = 0.5 * late
        take = 1.0 - keep
        before = jnp.maximum(s - 1, 0)
        square = [aux[p, rows(r), :] for p in PARITIES]
        right = mRy[s, 0, rows(r), :]
        now = [U[s, p, rows(r), :] for p in PARITIES]
        past = [U[before, p, rows(r), :] for p in PARITIES]
        rate = [dtr[p, rows(r), :] for p in PARITIES]
        yield
        right = shift_lanes(right, -1)
        square[1] = square[1] + right * right
        stores = []
        for p in PARITIES:
            inverse = lax.rsqrt(square[p])
            moved = now[p] - rate[p] * (square[p] * inverse)
            stores += [
                (rinv, (s, p, rows(r), slice(None)), inverse),
                (U, (s + 1, p, rows(r), slice(None)), keep * past[p] + take * moved),
            ]
        yield stores

    def forward_next(s, r):
        over = r + BLOCK >= forward_end(s)
        last = jnp.logical_and(over, s == STAGES - 1)
        done = r == IDLE
        s_next = jnp.where(over, jnp.minimum(s + 1, STAGES - 1), s)
        r_next = jnp.where(over, forward_start(s_next), r + BLOCK)
        r_next = jnp.where(jnp.logical_or(last, done), IDLE, r_next)
        return s_next, r_next

    forward_count = sum(-(-(forward_end(s) - forward_start(s)) // BLOCK) for s in range(STAGES))

    def forward_step(_, state):
        (s0, r0), (s1, r1), (s2, r2), (s3, r3) = state
        r0, r1, r2, r3 = aligned(r0), aligned(r1), aligned(r2), aligned(r3)
        together(advance(s3, r3), faces(s2, r2), columns_of(s0, r0))
        return (forward_next(s0, r0), (s0, r0), (s1, r1), (s2, r2))

    zero = jnp.int32(0)
    idle = jnp.int32(IDLE)
    lax.fori_loop(
        0,
        forward_count + 3,
        forward_step,
        ((zero, jnp.int32(forward_start(0))), (zero, idle), (zero, idle), (zero, idle)),
    )

    def weigh(s, r):
        loads = []
        for p in PARITIES:
            loads.append((
                g[p, rows(r), :],
                rinv[s, p, rows(r), :],
                rga[p, rows(r), :],
                dtr[p, rows(r), :],
                [U[s, p, rows(r, o), :] for o in (-1, 0, 1, 2)],
            ))
        yield
        stores = []
        for p in PARITIES:
            weight, inverse, total, rate, (um, u0, u1, u2) = loads[p]
            at = (p, rows(r), slice(None))
            w = (rate * weight) * inverse
            m0, m1, m2 = u0 - um, u1 - u0, u2 - u1
            d0, d1 = m1 - m0, m2 - m1
            stores += [
                (rga, at, total + weight * (1.0 / inverse)),
                (aux, at, w),
                (e6, at, (1.0 / 6.0) * (d1 - d0)),
                (tx, at, 0.5 * (d0 + d1)),
            ]
            if p == 1:
                stores.append((aux, (2, rows(r), slice(None)), shift_lanes(w, 1)))
        stores += [
            (win, (n, rows(r), slice(None)), value)
            for n, value in enumerate(window_of(loads[0][4][1], loads[1][4][1]))
        ]
        yield stores

    def face_adjoints(s, r):
        loads = []
        for p in PARITIES:
            loads.append((
                aux[p, rows(r), :],
                mLx[s, p, rows(r), :],
                aux[p, rows(r, -1), :],
                mRx[s, p, rows(r, -1), :],
                i1x[s, p, rows(r, -2), :], g2x[s, p, rows(r, -1), :], i3x[s, p, rows(r), :],
                [e6[p, rows(r, o), :] for o in (-2, -1, 0)],
                mLy[s, p, rows(r), :],
                aux[0 if p == 1 else 2, rows(r), :],
                mRy[s, p, rows(r), :],
                (i1y[s, p, rows(r), :], g2y[s, p, rows(r), :], i3y[s, p, rows(r), :]),
            ))
        window = load_window(s, r)
        yield
        stores = []
        for p in PARITIES:
            w, left, w1, right, i1, g2, i3, e = loads[p][:8]
            parts = face_adjoint(w * left, w1 * right, i1, g2, i3, e[0] - e[1], e[1] - e[2])
            stores += [(fx, (n, p, rows(r), slice(None)), part) for n, part in enumerate(parts)]
        _, e, t = third_differences(window)
        stores += [(ey, (n, rows(r), slice(None)), value) for n, value in enumerate(e + t)]
        for p in PARITIES:
            left, w1, right, terms = loads[p][8:]
            parts = face_adjoint(
                loads[p][0] * left, w1 * right, *terms,
                (1.0 / 6.0) * (e[p] - e[p + 1]), (1.0 / 6.0) * (e[p + 1] - e[p + 2]),
            )
            stores += [(fy, (n, p, rows(r), slice(None)), part) for n, part in enumerate(parts)]
        yield stores

    def rows_adjoint(s, r):
        e = [ey[n, rows(r), :] for n in range(4)]
        t = [ey[n + 4, rows(r), :] for n in range(4)]
        (g1e, g2e, g3e, f1e, f2e, bqe, bre, ame), (g1o, g2o, g3o, f1o, f2o, bqo, bro, amo) = (
            [fy[n, p, rows(r), :] for n in range(8)] for p in PARITIES
        )
        yield
        v0 = 4.0 * ((t[0] + e[0]) * g1e)
        v1o = 4.0 * ((t[1] + e[1]) * g1o)
        v1e = 4.0 * (t[1] * g2e)
        v2e = 4.0 * ((t[2] - e[2]) * g3e)
        v2o = 4.0 * (t[2] * g2o)
        v3 = 4.0 * ((t[3] - e[3]) * g3o)
        c = 13.0 / 3.0
        on_e = [
            (c * e[0]) * g1e + v0 + f1e,
            (c * e[1]) * (g2e + g1o) + v1o + ((f2e - f1e) + f1o),
            (c * e[2]) * (g3e + g2o) - v2e + ((f2o - f1o) - f2e),
            (c * e[3]) * g3o - v3 - f2o,
        ]
        on_t = [0.5 * v0, 0.5 * (v1e + v1o), 0.5 * (v2e + v2o), 0.5 * v3]
        lower = [b - a for a, b in zip(on_e, on_t)]
        upper = [b + a for a, b in zip(on_e, on_t)]
        d = [
            lower[0],
            lower[1] + upper[0] + bqe,
            lower[2] + upper[1] + (bre + bqo),
            lower[3] + upper[2] + bro,
            upper[3],
        ]
        m = [d[0] - d[1], (d[1] - d[2]) + ame, (d[2] - d[3]) + amo, d[3] - d[4]]
        u = [d[0], -d[0] - m[0], m[0] - m[1], m[1] - m[2], m[2] - m[3], m[3] - d[4], d[4]]
        even = u[3] + (shift_lanes(u[1], -1) + shift_lanes(u[5], 1))
        odd = u[4] + (shift_lanes(u[0], -2) + shift_lanes(u[2], -1)) + shift_lanes(u[6], 1)
        yield [(RT, (4, rows(r), slice(None)), even), (RT, (5, rows(r), slice(None)), odd)]

    def columns_adjoint(s, r):
        loads = []
        for p in PARITIES:
            loads.append((
                e6[p, rows(r), :],
                tx[p, rows(r), :],
                fx[0, p, rows(r, 2), :],
                fx[1, p, rows(r, 1), :],
                fx[2, p, rows(r), :],
                fx[3, p, rows(r, 2), :], fx[3, p, rows(r, 1), :], fx[4, p, rows(r, 1), :], fx[4, p, rows(r), :],
                fx[6, p, rows(r), :],
                fx[5, p, rows(r, 2), :],
            ))
        yield
        stores = []
        for p in PARITIES:
            e, t, g1, g2, g3, f12, f11, f21, f20, br, bq = loads[p]
            e = 6.0 * e
            v1 = (t + e) * g1
            v2 = t * g2
            v3 = (t - e) * g3
            on_e = ((13.0 / 3.0) * e) * ((g1 + g2) + g3) + 4.0 * (v1 - v3) + ((f12 - f11) + (f21 - f20))
            on_t = 2.0 * ((v1 + v2) + v3)
            stores += [
                (RT, (p, rows(r), slice(None)), (on_t - on_e) + br),
                (RT, (p + 2, rows(r), slice(None)), (on_t + on_e) + bq),
            ]
        yield stores

    def retreat(s, r):
        early = (1 - s % 2).astype(jnp.float32)
        scale = 1.0 - 0.5 * early
        loads = []
        for p in PARITIES:
            loads.append((
                [RT[p, rows(r, o), :] for o in (-1, 0, 1)],
                [RT[p + 2, rows(r, o - 1), :] for o in (-1, 0, 1)],
                fx[7, p, rows(r), :], fx[7, p, rows(r, 1), :],
                RT[4 + p, rows(r), :],
                g[p, rows(r), :],
                held[p, rows(r), :],
            ))
        yield
        stores = []
        for p in PARITIES:
            lower, upper, a0, a1, other, old, kept = loads[p]
            d = [a + b for a, b in zip(lower, upper)]
            back = (a0 - a1) + ((d[0] - d[1]) + (d[2] - d[1])) + other
            at = (p, rows(r), slice(None))
            stores += [(g, at, scale * ((old - back) + early * kept)), (held, at, old)]
        yield stores

    def backward_next(s, r):
        over = r + BLOCK >= backward_end(s)
        last = jnp.logical_and(over, s == 0)
        done = r == IDLE
        s_next = jnp.where(over, jnp.maximum(s - 1, 0), s)
        r_next = jnp.where(over, backward_start(s_next), r + BLOCK)
        r_next = jnp.where(jnp.logical_or(last, done), IDLE, r_next)
        return s_next, r_next

    backward_count = sum(-(-(backward_end(s) - backward_start(s)) // BLOCK) for s in range(STAGES))

    def backward_step(_, state):
        at = [(s, aligned(r)) for s, r in state]
        together(
            retreat(*at[5]), columns_adjoint(*at[3]), rows_adjoint(*at[2]), face_adjoints(*at[1]), weigh(*at[0])
        )
        return (backward_next(*state[0]),) + state[:5]

    last = jnp.int32(STAGES - 1)
    lax.fori_loop(
        0,
        backward_count + 5,
        backward_step,
        ((last, jnp.int32(backward_start(STAGES - 1))),) + ((last, idle),) * 5,
    )

    for n in range(3):
        for p in PARITIES:
            if n == 0:
                value = U[STAGES, p, own, :]
            elif n == 1:
                value = -DT * rga[p, own, :]
            else:
                value = 2.0 * g[p, own, :]
            stage_out[pl.ds(p, 128, stride=2), :] = value.T
        for device in range(16):
            out[device, n] = stage_out[16 * device : 16 * device + 16, :]


def sweep(core, from_left, from_right):
    full = (2, ROWS, 128)
    f32 = jnp.float32
    staged = pltpu.VMEM((STAGES,) + full, f32)
    plain = pltpu.VMEM(full, f32)
    return pl.pallas_call(
        kernel,
        out_shape=jax.ShapeDtypeStruct((16, 3, 16, 128), f32),
        in_specs=[pl.BlockSpec(memory_space=pltpu.VMEM)] * 3,
        out_specs=pl.BlockSpec(memory_space=pltpu.VMEM),
        scratch_shapes=[pltpu.VMEM((STAGES + 1,) + full, f32)]
        + [staged] * 11
        + [
            plain,
            plain,
            plain,
            plain,
            pltpu.VMEM((5, ROWS, 128), f32),
            plain,
            plain,
            pltpu.VMEM((3, ROWS, 128), f32),
            pltpu.VMEM((8,) + full, f32),
            pltpu.VMEM((8,) + full, f32),
            pltpu.VMEM((8, ROWS, 128), f32),
            pltpu.VMEM((6, ROWS, 128), f32),
            pltpu.VMEM((256, 128), f32),
        ],
        compiler_params=pltpu.CompilerParams(vmem_limit_bytes=63 * 2**20),
    )(core, from_left, from_right)


def turn_kernel(blocks, core, low, high, rows_ref):
    for n in range(3):
        for device in range(16):
            rows_ref[16 * device : 16 * device + 16, :] = blocks[device, n]
        for p in PARITIES:
            core[n, p] = rows_ref[pl.ds(p, 128, stride=2), :].T
    for p in PARITIES:
        for n, (width, start) in enumerate(((HALO, 0), (HALO, HALO), (HALO_COT, 2 * HALO))):
            low[p, start : start + width, :] = core[n, p, 0:width, :]
            high[p, start : start + width, :] = core[n, p, WIDTH - width : WIDTH, :]


def turn(blocks):
    f32 = jnp.float32
    edge = jax.ShapeDtypeStruct((2, 2 * HALO + HALO_COT, 128), f32)
    return pl.pallas_call(
        turn_kernel,
        out_shape=(jax.ShapeDtypeStruct((3, 2, 128, 128), f32), edge, edge),
        in_specs=[pl.BlockSpec(memory_space=pltpu.VMEM)],
        out_specs=[pl.BlockSpec(memory_space=pltpu.VMEM)] * 3,
        scratch_shapes=[pltpu.VMEM((256, 128), f32)],
    )(blocks)


def shards(level_set, spread_rate, cotangent):
    bands, runs = lax.axis_size("gy"), lax.axis_size("gx")
    stacked = jnp.stack([level_set, spread_rate, cotangent])
    blocks = stacked.reshape(3, 16, bands, WIDTH).transpose(2, 0, 1, 3)
    blocks = lax.all_to_all(blocks, "gy", 0, 0)
    core, low, high = turn(blocks)
    order = [(k, x) for x in range(runs) for k in range(bands)]
    place = [k * runs + x for k, x in order]
    up = list(zip(place, place[1:] + place[:1]))
    from_left = lax.ppermute(high, ("gy", "gx"), up)
    from_right = lax.ppermute(low, ("gy", "gx"), [(b, a) for a, b in up])
    done = lax.all_to_all(sweep(core, from_left, from_right), "gy", 0, 0)
    done = done.transpose(1, 2, 0, 3).reshape(3, 16, bands * WIDTH)
    return (done[0], done[1], done[2])


def solution(mesh):
    spec = P("gy", "gx")
    return jax.shard_map(
        shards, mesh=mesh, in_specs=(spec,) * 3, out_specs=(spec,) * 3, check_vma=False
    )
```

```python
import functools

import jax
import jax.numpy as jnp
from jax import lax
from jax.experimental import pallas as pl
from jax.experimental.pallas import tpu as pltpu
from jax.sharding import PartitionSpec as P

STEPS = 6
STAGES = 2 * STEPS
DT = 0.2
EPS = 0.001
FLOOR = 0.25

WIDTH = 128
HALO = 72
HALO_COT = 40
PAD = 16
BLOCK = 16
TILES = (WIDTH + 2 * HALO) // 8
OWN = PAD + HALO
IDLE = PAD + 2 * HALO + WIDTH + 16
ROWS = IDLE + BLOCK + 8
PARITIES = (0, 1)

FORWARD_WORK = (
    "mx0 mx1 dx0 dx1 ex0 ex1 odd_before even_after odd_after my0 my1 dy0 dy1 dy1_before "
    "ey0 ey1_before fc fa ey1 i1_0 i1_1 g2_1 sq0 sq1 right_after"
).split()
FACE_PARTS = "p1 g2 p3 f1 f2 h bq br dA".split()
AFTER = "p1_0 p1_1 g2_0 f1_0 f1_1 h_0 bq_0 dA_0".split()
BACKWARD_WORK = (
    "w0 w1 w1_before odd_before even_after odd_after ex0 ex1 tx0 tx1 ey0 ey1 ty0 ty1 fc ey1_before fa "
    "Rx0 Rx1 Tx0 Tx1 Dx0 Dx1 Ry0 Ry1 Qy0 Qy1 Dy0 Dy1 Dy1_before Dy0_after"
).split()
BACKWARD_WORK += [f"{d}{n}_{p}" for d in "xy" for n in FACE_PARTS for p in PARITIES] + ["after_" + n for n in AFTER]
SLOTS = max(len(FORWARD_WORK), len(BACKWARD_WORK))


def shift_lanes(value, by):
    return pltpu.roll(value, by % 128, 1)


def smoothness(e, t):
    h = EPS + (13.0 / 12.0 * e) * e
    plus, minus = t + e, t - e
    return h + plus * plus, h + t * t, h + minus * minus


def face_values(m, q, r, i1, g2, i3, f1, f2):
    x, y = g2 * i1, g2 * i3
    x, y = x * x, y * y
    a, b = x * f1, y * f2
    s = a + b
    s = s + s
    total = (x + y) + 6.0
    six = 6.0 * m
    p = q + r
    left = ((six + p) + r) + (s + b) * (1.0 / (total + (y + y)))
    right = ((p - six) + q) + (s + a) * (1.0 / (total + (x + x)))
    return jnp.maximum(left, 0.0), jnp.maximum(right, 0.0)


def face_adjoint(aL, aR, i1, g2, i3, f1, f2):
    x, y = g2 * i1, g2 * i3
    x, y = x * x, y * y
    a, b = x * f1, y * f2
    s = a + b
    s = s + s
    total = (x + y) + 6.0
    kL = 1.0 / (total + (y + y))
    kR = 1.0 / (total + (x + x))
    bL, bR = aL * kL, aR * kR
    cL = bL * ((s + b) * kL)
    cR = bR * ((s + a) * kR)
    both = bL + bR
    both = both + both
    on_a, on_b = both + bR, both + bL
    gX = a * on_a - x * (cL + 3.0 * cR)
    gY = b * on_b - y * (3.0 * cL + cR)
    gf1, gf2 = x * on_a, y * on_b
    aS = aL + aR
    return dict(
        p1=gX * i1, g2=(gX + gY) * (1.0 / g2), p3=gY * i3,
        f1=gf1, f2=gf2, h=gf2 - gf1,
        bq=aS + aR, br=aS + aL, dA=aL - aR,
    )


def smoothness_adjoint(e, t, p1, g2, p3, f1, h, f2):
    v1, v2, v3 = (t + e) * p1, t * g2, (t - e) * p3
    on_e = ((13.0 / 3.0) * e) * (g2 - (p1 + p3)) + 4.0 * (v3 - v1) + ((f1 + h) - f2)
    on_t = 2.0 * (v2 - (v1 + v3))
    return on_t - on_e, on_t + on_e


def forward_start(s):
    return PAD + 8 * ((3 * (s + 1)) // 8) - 8


def forward_end(s):
    return PAD + 8 * (TILES - (3 * (s + 1)) // 8) + 8


def backward_start(s):
    return PAD + 8 * ((39 + 3 * (STAGES - 1 - s)) // 8) - 8


def backward_end(s):
    return PAD + 8 * (TILES - (39 + 3 * (STAGES - 1 - s)) // 8) + 8


def kernel(core, from_left, from_right, out, U, i1x, g2x, i3x, mLx, mRx, i1y, g2y, i3y, mLy, mRy, rinv, rate, g, held, rga, stage_out, *work):
    own = slice(OWN, OWN + WIDTH)
    low = slice(PAD, PAD + HALO)
    high = slice(OWN + WIDTH, OWN + WIDTH + HALO)
    held[...] = jnp.zeros_like(held)
    rga[...] = jnp.zeros_like(rga)
    for p in PARITIES:
        U[0, p, own, :] = core[0, p]
        U[0, p, low, :] = from_left[p, 0:HALO, :]
        U[0, p, high, :] = from_right[p, 0:HALO, :]
        rate[p, own, :] = (DT / 6.0) * core[1, p]
        rate[p, low, :] = (DT / 6.0) * from_left[p, HALO : 2 * HALO, :]
        rate[p, high, :] = (DT / 6.0) * from_right[p, HALO : 2 * HALO, :]
        g[p, own, :] = 0.5 * core[2, p]
        g[p, OWN - HALO_COT : OWN, :] = 0.5 * from_left[p, 2 * HALO :, :]
        g[p, OWN + WIDTH : OWN + WIDTH + HALO_COT, :] = 0.5 * from_right[p, 2 * HALO :, :]

    def rows(r, offset=0):
        return pl.ds(r + offset, BLOCK)

    def aligned(r):
        return pl.multiple_of(r, 8)

    def together(*phases):
        for phase in phases:
            next(phase)
        stores = [store for phase in phases for store in next(phase)]
        for ref, index, value in stores:
            ref[index] = value

    def at(r, *lead):
        return lead + (rows(r), slice(None))

    def tools(names):
        slot = {name: n for n, name in enumerate(names)}

        def load(name, r, offset=0):
            return work[slot[name]][rows(r, offset), :]

        def put(name, r, value):
            return (work[slot[name]], at(r), value)

        return load, put

    load, put = tools(FORWARD_WORK)

    def differences(s, r):
        us = [[U[s, p, rows(r, o), :] for o in (-1, 0, 1)] for p in PARITIES]
        yield
        stores = []
        for p in PARITIES:
            um, u0, u1 = us[p]
            m0, m1 = u0 - um, u1 - u0
            stores += [put(f"mx{p}", r, m0), put(f"dx{p}", r, m1 - m0)]
        even, odd = us[0][1], us[1][1]
        stores += [
            put("odd_before", r, shift_lanes(odd, 1)),
            put("even_after", r, shift_lanes(even, -1)),
            put("odd_after", r, shift_lanes(odd, -1)),
        ]
        yield stores

    def smooth_columns(s, r):
        ds = [[load(f"dx{p}", r, o) for o in (0, 1)] for p in PARITIES]
        yield
        stores = []
        for p in PARITIES:
            d0, d1 = ds[p]
            e = d1 - d0
            s1, s2, s3 = smoothness(e, 0.5 * (d0 + d1))
            stores += [
                (i1x, at(r, s, p), 1.0 / s1),
                (g2x, at(r, s, p), s2),
                (i3x, at(r, s, p), 1.0 / s3),
                put(f"ex{p}", r, e),
            ]
        yield stores

    def smooth_rows(s, r):
        even, odd = (U[s, p, rows(r), :] for p in PARITIES)
        odd_before, even_after, odd_after = (load(n, r) for n in ("odd_before", "even_after", "odd_after"))
        yield
        m = [even - odd_before, odd - even, even_after - odd, odd_after - even_after]
        d = [b - a for a, b in zip(m[:-1], m[1:])]
        e = [b - a for a, b in zip(d[:-1], d[1:])]
        terms = [smoothness(e[p], 0.5 * (d[p] + d[p + 1])) for p in PARITIES]
        stores = []
        for p in PARITIES:
            stores += [
                put(f"my{p}", r, m[p]),
                put(f"dy{p}", r, d[p]),
                put(f"ey{p}", r, e[p]),
                put(f"i1_{p}", r, 1.0 / terms[p][0]),
                (i3y, at(r, s, p), 1.0 / terms[p][2]),
            ]
        stores += [(g2y, at(r, s, 1), terms[0][1]), put("g2_1", r, terms[1][1]), put("fc", r, e[0] - e[1])]
        yield stores

    def shift_rows(s, r):
        names = ("i1_0", "i1_1", "g2_1", "dy1", "ey1", "fc")
        values = [load(name, r) for name in names]
        yield
        i10, i11, g21, dy1, ey1, fc = (shift_lanes(value, 1) for value in values)
        yield [
            (i1y, at(r, s, 0), i10),
            (i1y, at(r, s, 1), i11),
            (g2y, at(r, s, 0), g21),
            put("dy1_before", r, dy1),
            put("ey1_before", r, ey1),
            put("fa", r, fc),
        ]

    def faces(s, r):
        columns = []
        for p in PARITIES:
            columns.append((
                load(f"mx{p}", r),
                load(f"dx{p}", r, -1),
                load(f"dx{p}", r),
                i1x[s, p, rows(r, -2), :], g2x[s, p, rows(r, -1), :], i3x[s, p, rows(r), :],
                [load(f"ex{p}", r, o) for o in (-2, -1, 0)],
            ))
        terms = [(i1y[s, p, rows(r), :], g2y[s, p, rows(r), :], i3y[s, p, rows(r), :]) for p in PARITIES]
        my = [load("my0", r), load("my1", r)]
        dy = [load("dy1_before", r), load("dy0", r), load("dy1", r)]
        fa, fc = load("fa", r), load("fc", r)
        ey1_before, ey0 = load("ey1_before", r), load("ey0", r)
        yield
        stores = []
        fb = ey1_before - ey0
        f = (fa, fb, fc)
        for p in PARITIES:
            m, q, rr, i1, g2, i3, e = columns[p]
            left, right = face_values(m, q, rr, i1, g2, i3, e[0] - e[1], e[1] - e[2])
            stores += [(mLx, at(r, s, p), left), (mRx, at(r, s, p), right)]
            square = left * left
            left, right = face_values(my[p], dy[p], dy[p + 1], *terms[p], f[p], f[p + 1])
            stores += [(mLy, at(r, s, p), left), (mRy, at(r, s, p), right)]
            stores.append(put(f"sq{p}", r, (square + left * left) + 36.0 * FLOOR))
        yield stores

    def shift_right(s, r):
        right = mRy[s, 0, rows(r), :]
        yield
        yield [put("right_after", r, shift_lanes(right, -1))]

    def advance(s, r):
        late = (s % 2).astype(jnp.float32)
        keep = 0.5 * late
        take = 1.0 - keep
        before = jnp.maximum(s - 1, 0)
        square = [load(f"sq{p}", r) for p in PARITIES]
        rights = [mRy[s, 1, rows(r), :], load("right_after", r)]
        columns = [mRx[s, p, rows(r, 1), :] for p in PARITIES]
        now = [U[s, p, rows(r), :] for p in PARITIES]
        past = [U[before, p, rows(r), :] for p in PARITIES]
        rates = [rate[p, rows(r), :] for p in PARITIES]
        yield
        stores = []
        for p in PARITIES:
            total = square[p] + (rights[p] * rights[p] + columns[p] * columns[p])
            inverse = lax.rsqrt(total)
            moved = now[p] - rates[p] * (total * inverse)
            stores += [
                (rinv, at(r, s, p), inverse),
                (U, at(r, s + 1, p), keep * past[p] + take * moved),
            ]
        yield stores

    def forward_next(s, r):
        over = r + BLOCK >= forward_end(s)
        last = jnp.logical_and(over, s == STAGES - 1)
        done = r == IDLE
        s_next = jnp.where(over, jnp.minimum(s + 1, STAGES - 1), s)
        r_next = jnp.where(over, forward_start(s_next), r + BLOCK)
        r_next = jnp.where(jnp.logical_or(last, done), IDLE, r_next)
        return s_next, r_next

    forward_count = sum(-(-(forward_end(s) - forward_start(s)) // BLOCK) for s in range(STAGES))

    def forward_step(_, state):
        lag = [(s, aligned(r)) for s, r in state]
        together(
            advance(*lag[6]),
            shift_right(*lag[5]),
            faces(*lag[4]),
            shift_rows(*lag[2]),
            smooth_columns(*lag[2]),
            smooth_rows(*lag[1]),
            differences(*lag[0]),
        )
        return (forward_next(*state[0]),) + state[:6]

    zero = jnp.int32(0)
    idle = jnp.int32(IDLE)
    lax.fori_loop(
        0,
        forward_count + 6,
        forward_step,
        ((zero, jnp.int32(forward_start(0))),) + ((zero, idle),) * 6,
    )

    load, put = tools(BACKWARD_WORK)

    def weigh(s, r):
        loads = []
        for p in PARITIES:
            loads.append((
                g[p, rows(r), :],
                rinv[s, p, rows(r), :],
                rga[p, rows(r), :],
                rate[p, rows(r), :],
                [U[s, p, rows(r, o), :] for o in (-1, 0, 1, 2)],
            ))
        yield
        stores = []
        for p in PARITIES:
            weight, inverse, total, rates, (um, u0, u1, u2) = loads[p]
            m0, m1, m2 = u0 - um, u1 - u0, u2 - u1
            d0, d1 = m1 - m0, m2 - m1
            stores += [
                (rga, at(r, p), total + weight * (1.0 / inverse)),
                put(f"w{p}", r, (rates * weight) * inverse),
                put(f"ex{p}", r, d1 - d0),
                put(f"tx{p}", r, 0.5 * (d0 + d1)),
            ]
        even, odd = loads[0][4][1], loads[1][4][1]
        stores += [
            put("odd_before", r, shift_lanes(odd, 1)),
            put("even_after", r, shift_lanes(even, -1)),
            put("odd_after", r, shift_lanes(odd, -1)),
        ]
        yield stores

    def differ_rows(s, r):
        even, odd = (U[s, p, rows(r), :] for p in PARITIES)
        odd_before, even_after, odd_after = (load(n, r) for n in ("odd_before", "even_after", "odd_after"))
        yield
        m = [even - odd_before, odd - even, even_after - odd, odd_after - even_after]
        d = [b - a for a, b in zip(m[:-1], m[1:])]
        e = [b - a for a, b in zip(d[:-1], d[1:])]
        stores = [put("fc", r, e[0] - e[1])]
        for p in PARITIES:
            stores += [put(f"ey{p}", r, e[p]), put(f"ty{p}", r, 0.5 * (d[p] + d[p + 1]))]
        yield stores

    def shift_before(s, r):
        pairs = (("ey1", "ey1_before"), ("fc", "fa"), ("w1", "w1_before"))
        values = [load(name, r) for name, _ in pairs]
        yield
        yield [put(name, r, shift_lanes(value, 1)) for (_, name), value in zip(pairs, values)]

    def face_adjoints(s, r):
        loads = []
        for p in PARITIES:
            loads.append((
                load(f"w{p}", r), mLx[s, p, rows(r), :],
                load(f"w{p}", r, -1), mRx[s, p, rows(r), :],
                (i1x[s, p, rows(r, -2), :], g2x[s, p, rows(r, -1), :], i3x[s, p, rows(r), :]),
                [load(f"ex{p}", r, o) for o in (-2, -1, 0)],
                mLy[s, p, rows(r), :],
                load("w0" if p == 1 else "w1_before", r), mRy[s, p, rows(r), :],
                (i1y[s, p, rows(r), :], g2y[s, p, rows(r), :], i3y[s, p, rows(r), :]),
            ))
        fa, fc = load("fa", r), load("fc", r)
        ey1_before, ey0 = load("ey1_before", r), load("ey0", r)
        yield
        stores = []
        f = (fa, ey1_before - ey0, fc)
        for p in PARITIES:
            w, leftx, wx, rightx, terms, e, lefty, wy, righty, termsy = loads[p]
            parts = face_adjoint(w * leftx, wx * rightx, *terms, e[0] - e[1], e[1] - e[2])
            stores += [put(f"x{n}_{p}", r, part) for n, part in parts.items()]
            parts = face_adjoint(w * lefty, wy * righty, *termsy, f[p], f[p + 1])
            stores += [put(f"y{n}_{p}", r, part) for n, part in parts.items()]
        yield stores

    def shift_after(s, r):
        values = [load("y" + name, r) for name in AFTER]
        yield
        yield [put("after_" + name, r, shift_lanes(value, -1)) for name, value in zip(AFTER, values)]

    def rows_adjoint(s, r):
        loads = []
        for p in PARITIES:
            ahead = (lambda n: load(f"y{n}_1", r)) if p == 0 else (lambda n: load(f"after_{n}_0", r))
            loads.append((
                load(f"ey{p}", r), load(f"ty{p}", r),
                load(f"after_p1_{p}", r), ahead("g2"), load(f"yp3_{p}", r),
                load(f"after_f1_{p}", r), ahead("h"), load(f"yf2_{p}", r),
                load(f"ybr_{p}", r), ahead("bq"),
            ))
        yield
        stores = []
        for p in PARITIES:
            lower, upper = smoothness_adjoint(*loads[p][:8])
            stores += [put(f"Ry{p}", r, lower + (loads[p][8] + loads[p][9])), put(f"Qy{p}", r, upper)]
        yield stores

    def columns_adjoint(s, r):
        loads = []
        for p in PARITIES:
            loads.append((
                load(f"ex{p}", r), load(f"tx{p}", r),
                load(f"xp1_{p}", r, 2), load(f"xg2_{p}", r, 1), load(f"xp3_{p}", r),
                load(f"xf1_{p}", r, 2), load(f"xh_{p}", r, 1), load(f"xf2_{p}", r),
                load(f"xbr_{p}", r), load(f"xbq_{p}", r, 2),
            ))
        yield
        stores = []
        for p in PARITIES:
            lower, upper = smoothness_adjoint(*loads[p][:8])
            stores += [put(f"Rx{p}", r, lower + loads[p][8]), put(f"Tx{p}", r, upper + loads[p][9])]
        yield stores

    def second_adjoint(s, r):
        columns = [(load(f"Rx{p}", r), load(f"Tx{p}", r, -1)) for p in PARITIES]
        lower = [load(f"Ry{p}", r) for p in PARITIES]
        upper = [load(f"Qy{p}", r) for p in PARITIES]
        yield
        stores = [put(f"Dx{p}", r, columns[p][0] + columns[p][1]) for p in PARITIES]
        stores += [put("Dy0", r, lower[0] + shift_lanes(upper[1], 1)), put("Dy1", r, lower[1] + upper[0])]
        yield stores

    def shift_second(s, r):
        d0, d1 = load("Dy0", r), load("Dy1", r)
        yield
        yield [put("Dy0_after", r, shift_lanes(d0, -1)), put("Dy1_before", r, shift_lanes(d1, 1))]

    def retreat(s, r):
        early = (1 - s % 2).astype(jnp.float32)
        scale = 1.0 - 0.5 * early
        loads = []
        for p in PARITIES:
            loads.append((
                [load(f"Dx{p}", r, o) for o in (-1, 0, 1)],
                [load(n, r) for n in (("Dy1_before", "Dy0", "Dy1") if p == 0 else ("Dy0", "Dy1", "Dy0_after"))],
                load(f"xdA_{p}", r), load(f"xdA_{p}", r, 1),
                load(f"ydA_{p}", r), load("ydA_1" if p == 0 else "after_dA_0", r),
                g[p, rows(r), :],
                held[p, rows(r), :],
            ))
        yield
        stores = []
        for p in PARITIES:
            dx, dy, ax0, ax1, ay0, ay1, old, kept = loads[p]
            back = 6.0 * ((ax0 - ax1) + (ay0 - ay1))
            back = back + ((dx[0] - dx[1]) + (dx[2] - dx[1]))
            back = back + ((dy[0] - dy[1]) + (dy[2] - dy[1]))
            stores += [(g, at(r, p), scale * ((old - back) + early * kept)), (held, at(r, p), old)]
        yield stores

    def backward_next(s, r):
        over = r + BLOCK >= backward_end(s)
        last = jnp.logical_and(over, s == 0)
        done = r == IDLE
        s_next = jnp.where(over, jnp.maximum(s - 1, 0), s)
        r_next = jnp.where(over, backward_start(s_next), r + BLOCK)
        r_next = jnp.where(jnp.logical_or(last, done), IDLE, r_next)
        return s_next, r_next

    backward_count = sum(-(-(backward_end(s) - backward_start(s)) // BLOCK) for s in range(STAGES))

    def backward_step(_, state):
        lag = [(s, aligned(r)) for s, r in state]
        together(
            retreat(*lag[8]),
            shift_second(*lag[7]),
            second_adjoint(*lag[6]),
            columns_adjoint(*lag[5]),
            rows_adjoint(*lag[5]),
            shift_after(*lag[4]),
            face_adjoints(*lag[3]),
            shift_before(*lag[2]),
            differ_rows(*lag[1]),
            weigh(*lag[0]),
        )
        return (backward_next(*state[0]),) + state[:8]

    last = jnp.int32(STAGES - 1)
    lax.fori_loop(
        0,
        backward_count + 8,
        backward_step,
        ((last, jnp.int32(backward_start(STAGES - 1))),) + ((last, idle),) * 8,
    )

    for n in range(3):
        for p in PARITIES:
            if n == 0:
                value = U[STAGES, p, own, :]
            elif n == 1:
                value = (-DT / 6.0) * rga[p, own, :]
            else:
                value = 2.0 * g[p, own, :]
            stage_out[pl.ds(p, 128, stride=2), :] = value.T
        for device in range(16):
            out[device, n] = stage_out[16 * device : 16 * device + 16, :]


def sweep(core, from_left, from_right):
    full = (2, ROWS, 128)
    f32 = jnp.float32
    staged = pltpu.VMEM((STAGES,) + full, f32)
    plain = pltpu.VMEM(full, f32)
    return pl.pallas_call(
        kernel,
        out_shape=jax.ShapeDtypeStruct((16, 3, 16, 128), f32),
        in_specs=[pl.BlockSpec(memory_space=pltpu.VMEM)] * 3,
        out_specs=pl.BlockSpec(memory_space=pltpu.VMEM),
        scratch_shapes=[pltpu.VMEM((STAGES + 1,) + full, f32)]
        + [staged] * 11
        + [plain] * 4
        + [
            pltpu.VMEM((256, 128), f32),
        ]
        + [pltpu.VMEM((ROWS, 128), f32)] * SLOTS,
        compiler_params=pltpu.CompilerParams(vmem_limit_bytes=63 * 2**20),
    )(core, from_left, from_right)


def turn_kernel(blocks, core, low, high, rows_ref):
    for n in range(3):
        for device in range(16):
            rows_ref[16 * device : 16 * device + 16, :] = blocks[device, n]
        for p in PARITIES:
            core[n, p] = rows_ref[pl.ds(p, 128, stride=2), :].T
    for p in PARITIES:
        for n, (width, start) in enumerate(((HALO, 0), (HALO, HALO), (HALO_COT, 2 * HALO))):
            low[p, start : start + width, :] = core[n, p, 0:width, :]
            high[p, start : start + width, :] = core[n, p, WIDTH - width : WIDTH, :]


def turn(blocks):
    f32 = jnp.float32
    edge = jax.ShapeDtypeStruct((2, 2 * HALO + HALO_COT, 128), f32)
    return pl.pallas_call(
        turn_kernel,
        out_shape=(jax.ShapeDtypeStruct((3, 2, 128, 128), f32), edge, edge),
        in_specs=[pl.BlockSpec(memory_space=pltpu.VMEM)],
        out_specs=[pl.BlockSpec(memory_space=pltpu.VMEM)] * 3,
        scratch_shapes=[pltpu.VMEM((256, 128), f32)],
    )(blocks)


CHAIN = (0, 1, 5, 4, 8, 9, 13, 12, 14, 15, 11, 10, 6, 7, 3, 2)


def columns_held(device):
    place = CHAIN.index(device)
    backwards = lax.axis_index("gx") % 2
    strip = place + backwards * (len(CHAIN) - 1 - 2 * place)
    return pl.ds(pl.multiple_of(strip * WIDTH, WIDTH), WIDTH)


def pack_kernel(level_set, spread_rate, cotangent, blocks):
    for device in range(len(CHAIN)):
        columns = columns_held(device)
        for n, ref in enumerate((level_set, spread_rate, cotangent)):
            blocks[device, n] = ref[:, columns]


def unpack_kernel(blocks, final_state, rate_gradient, initial_gradient):
    for device in range(len(CHAIN)):
        columns = columns_held(device)
        for n, ref in enumerate((final_state, rate_gradient, initial_gradient)):
            ref[:, columns] = blocks[device, n]


def shards(level_set, spread_rate, cotangent):
    bands, runs = lax.axis_size("gy"), lax.axis_size("gx")
    vmem = pl.BlockSpec(memory_space=pltpu.VMEM)
    block = jax.ShapeDtypeStruct(level_set.shape, jnp.float32)
    blocks = pl.pallas_call(
        pack_kernel,
        out_shape=jax.ShapeDtypeStruct((bands, 3, level_set.shape[0], WIDTH), jnp.float32),
        in_specs=[vmem] * 3,
        out_specs=vmem,
    )(level_set, spread_rate, cotangent)
    blocks = lax.all_to_all(blocks, "gy", 0, 0)
    core, low, high = turn(blocks)
    place = [k * runs + x for x in range(runs) for k in (CHAIN if x % 2 == 0 else CHAIN[::-1])]
    up = list(zip(place, place[1:] + place[:1]))
    from_left = lax.ppermute(high, ("gy", "gx"), up)
    from_right = lax.ppermute(low, ("gy", "gx"), [(b, a) for a, b in up])
    done = lax.all_to_all(sweep(core, from_left, from_right), "gy", 0, 0)
    return pl.pallas_call(
        unpack_kernel,
        out_shape=(block,) * 3,
        in_specs=[vmem],
        out_specs=(vmem,) * 3,
    )(done)


def solution(mesh):
    spec = P("gy", "gx")
    return jax.shard_map(
        shards, mesh=mesh, in_specs=(spec,) * 3, out_specs=(spec,) * 3, check_vma=False
    )
```

```python
import functools

import jax
import jax.numpy as jnp
from jax import lax
from jax.experimental import pallas as pl
from jax.experimental.pallas import tpu as pltpu
from jax.sharding import PartitionSpec as P

STEPS = 6
STAGES = 2 * STEPS
DT = 0.2
EPS = 0.001
FLOOR = 0.25

WIDTH = 128
HALO = 72
HALO_COT = 40
PAD = 16
BLOCK = 16
TILES = (WIDTH + 2 * HALO) // 8
OWN = PAD + HALO
IDLE = PAD + 2 * HALO + WIDTH + 16
ROWS = IDLE + BLOCK + 8
PARITIES = (0, 1)

FORWARD_WORK = (
    "mx0", "mx1", "dx0", "dx1", "ex0", "ex1", "odd_before", "even_after", "odd_after", "my0", "my1", "dy0",
    "dy1", "dy1_before", "ey0", "ey1_before", "fc", "fa", "ey1", "i1_0", "i1_1", "g2_1", "sq0", "sq1",
    "right_after",
)
FACE_PARTS = (
    "p1", "g2", "p3", "f1", "f2", "h", "bq", "br", "dA",
)
AFTER = (
    "p1_0", "p1_1", "g2_0", "f1_0", "f1_1", "h_0", "bq_0", "dA_0",
)
BACKWARD_WORK = (
    "w0", "w1", "w1_before", "odd_before", "even_after", "odd_after", "ex0", "ex1", "tx0", "tx1", "ey0", "ey1",
    "ty0", "ty1", "fc", "ey1_before", "fa", "Rx0", "Rx1", "Tx0", "Tx1", "Dx0", "Dx1", "Ry0", "Ry1", "Qy0",
    "Qy1", "Dy0", "Dy1", "Dy1_before", "Dy0_after",
)
BACKWARD_WORK += tuple(f"{d}{n}_{p}" for d in "xy" for n in FACE_PARTS for p in PARITIES)
BACKWARD_WORK += tuple("after_" + n for n in AFTER)
SLOTS = max(len(FORWARD_WORK), len(BACKWARD_WORK))


def shift_lanes(value, by):
    return pltpu.roll(value, by % 128, 1)


def smoothness(e, t):
    h = EPS + (13.0 / 12.0 * e) * e
    plus, minus = t + e, t - e
    return h + plus * plus, h + t * t, h + minus * minus


def face_values(m, q, r, i1, g2, i3, f1, f2):
    x, y = g2 * i1, g2 * i3
    x, y = x * x, y * y
    a, b = x * f1, y * f2
    s = a + b
    s = s + s
    total = (x + y) + 6.0
    six = 6.0 * m
    p = q + r
    left = ((six + p) + r) + (s + b) * (1.0 / (total + (y + y)))
    right = ((p - six) + q) + (s + a) * (1.0 / (total + (x + x)))
    return jnp.maximum(left, 0.0), jnp.maximum(right, 0.0)


def face_adjoint(aL, aR, i1, g2, i3, f1, f2):
    x, y = g2 * i1, g2 * i3
    x, y = x * x, y * y
    a, b = x * f1, y * f2
    s = a + b
    s = s + s
    total = (x + y) + 6.0
    kL = 1.0 / (total + (y + y))
    kR = 1.0 / (total + (x + x))
    bL, bR = aL * kL, aR * kR
    cL = bL * ((s + b) * kL)
    cR = bR * ((s + a) * kR)
    both = bL + bR
    both = both + both
    on_a, on_b = both + bR, both + bL
    gX = a * on_a - x * (cL + 3.0 * cR)
    gY = b * on_b - y * (3.0 * cL + cR)
    gf1, gf2 = x * on_a, y * on_b
    aS = aL + aR
    return dict(
        p1=gX * i1, g2=(gX + gY) * (1.0 / g2), p3=gY * i3,
        f1=gf1, f2=gf2, h=gf2 - gf1,
        bq=aS + aR, br=aS + aL, dA=aL - aR,
    )


def smoothness_adjoint(e, t, p1, g2, p3, f1, h, f2):
    v1, v2, v3 = (t + e) * p1, t * g2, (t - e) * p3
    on_e = ((13.0 / 3.0) * e) * (g2 - (p1 + p3)) + 4.0 * (v3 - v1) + ((f1 + h) - f2)
    on_t = 2.0 * (v2 - (v1 + v3))
    return on_t - on_e, on_t + on_e


def forward_start(s):
    return PAD + 8 * ((3 * (s + 1)) // 8) - 8


def forward_end(s):
    return PAD + 8 * (TILES - (3 * (s + 1)) // 8) + 8


def backward_start(s):
    return PAD + 8 * ((39 + 3 * (STAGES - 1 - s)) // 8) - 8


def backward_end(s):
    return PAD + 8 * (TILES - (39 + 3 * (STAGES - 1 - s)) // 8) + 8


def kernel(core, from_left, from_right, out, U, i1x, g2x, i3x, mLx, mRx, i1y, g2y, i3y, mLy, mRy, rinv, rate, g, held, rga, stage_out, *work):
    own = slice(OWN, OWN + WIDTH)
    low = slice(PAD, PAD + HALO)
    high = slice(OWN + WIDTH, OWN + WIDTH + HALO)
    held[...] = jnp.zeros_like(held)
    rga[...] = jnp.zeros_like(rga)
    for p in PARITIES:
        U[0, p, own, :] = core[0, p]
        U[0, p, low, :] = from_left[p, 0:HALO, :]
        U[0, p, high, :] = from_right[p, 0:HALO, :]
        rate[p, own, :] = (DT / 6.0) * core[1, p]
        rate[p, low, :] = (DT / 6.0) * from_left[p, HALO : 2 * HALO, :]
        rate[p, high, :] = (DT / 6.0) * from_right[p, HALO : 2 * HALO, :]
        g[p, own, :] = 0.5 * core[2, p]
        g[p, OWN - HALO_COT : OWN, :] = 0.5 * from_left[p, 2 * HALO :, :]
        g[p, OWN + WIDTH : OWN + WIDTH + HALO_COT, :] = 0.5 * from_right[p, 2 * HALO :, :]

    def rows(r, offset=0):
        return pl.ds(r + offset, BLOCK)

    def aligned(r):
        return pl.multiple_of(r, 8)

    def together(*phases):
        for phase in phases:
            next(phase)
        stores = [store for phase in phases for store in next(phase)]
        for ref, index, value in stores:
            ref[index] = value

    def at(r, *lead):
        return lead + (rows(r), slice(None))

    def tools(names):
        slot = {name: n for n, name in enumerate(names)}

        def load(name, r, offset=0):
            return work[slot[name]][rows(r, offset), :]

        def put(name, r, value):
            return (work[slot[name]], at(r), value)

        return load, put

    load, put = tools(FORWARD_WORK)

    def differences(s, r):
        us = [[U[s, p, rows(r, o), :] for o in (-1, 0, 1)] for p in PARITIES]
        yield
        stores = []
        for p in PARITIES:
            um, u0, u1 = us[p]
            m0, m1 = u0 - um, u1 - u0
            stores += [put(f"mx{p}", r, m0), put(f"dx{p}", r, m1 - m0)]
        even, odd = us[0][1], us[1][1]
        stores += [
            put("odd_before", r, shift_lanes(odd, 1)),
            put("even_after", r, shift_lanes(even, -1)),
            put("odd_after", r, shift_lanes(odd, -1)),
        ]
        yield stores

    def smooth_columns(s, r):
        ds = [[load(f"dx{p}", r, o) for o in (0, 1)] for p in PARITIES]
        yield
        stores = []
        for p in PARITIES:
            d0, d1 = ds[p]
            e = d1 - d0
            s1, s2, s3 = smoothness(e, 0.5 * (d0 + d1))
            stores += [
                (i1x, at(r, s, p), 1.0 / s1),
                (g2x, at(r, s, p), s2),
                (i3x, at(r, s, p), 1.0 / s3),
                put(f"ex{p}", r, e),
            ]
        yield stores

    def smooth_rows(s, r):
        even, odd = (U[s, p, rows(r), :] for p in PARITIES)
        odd_before, even_after, odd_after = (load(n, r) for n in ("odd_before", "even_after", "odd_after"))
        yield
        m = [even - odd_before, odd - even, even_after - odd, odd_after - even_after]
        d = [b - a for a, b in zip(m[:-1], m[1:])]
        e = [b - a for a, b in zip(d[:-1], d[1:])]
        terms = [smoothness(e[p], 0.5 * (d[p] + d[p + 1])) for p in PARITIES]
        stores = []
        for p in PARITIES:
            stores += [
                put(f"my{p}", r, m[p]),
                put(f"dy{p}", r, d[p]),
                put(f"ey{p}", r, e[p]),
                put(f"i1_{p}", r, 1.0 / terms[p][0]),
                (i3y, at(r, s, p), 1.0 / terms[p][2]),
            ]
        stores += [(g2y, at(r, s, 1), terms[0][1]), put("g2_1", r, terms[1][1]), put("fc", r, e[0] - e[1])]
        yield stores

    def shift_rows(s, r):
        names = ("i1_0", "i1_1", "g2_1", "dy1", "ey1", "fc")
        values = [load(name, r) for name in names]
        yield
        i10, i11, g21, dy1, ey1, fc = (shift_lanes(value, 1) for value in values)
        yield [
            (i1y, at(r, s, 0), i10),
            (i1y, at(r, s, 1), i11),
            (g2y, at(r, s, 0), g21),
            put("dy1_before", r, dy1),
            put("ey1_before", r, ey1),
            put("fa", r, fc),
        ]

    def faces(s, r):
        columns = []
        for p in PARITIES:
            columns.append((
                load(f"mx{p}", r),
                load(f"dx{p}", r, -1),
                load(f"dx{p}", r),
                i1x[s, p, rows(r, -2), :], g2x[s, p, rows(r, -1), :], i3x[s, p, rows(r), :],
                [load(f"ex{p}", r, o) for o in (-2, -1, 0)],
            ))
        terms = [(i1y[s, p, rows(r), :], g2y[s, p, rows(r), :], i3y[s, p, rows(r), :]) for p in PARITIES]
        my = [load("my0", r), load("my1", r)]
        dy = [load("dy1_before", r), load("dy0", r), load("dy1", r)]
        fa, fc = load("fa", r), load("fc", r)
        ey1_before, ey0 = load("ey1_before", r), load("ey0", r)
        yield
        stores = []
        fb = ey1_before - ey0
        f = (fa, fb, fc)
        for p in PARITIES:
            m, q, rr, i1, g2, i3, e = columns[p]
            left, right = face_values(m, q, rr, i1, g2, i3, e[0] - e[1], e[1] - e[2])
            stores += [(mLx, at(r, s, p), left), (mRx, at(r, s, p), right)]
            square = left * left
            left, right = face_values(my[p], dy[p], dy[p + 1], *terms[p], f[p], f[p + 1])
            stores += [(mLy, at(r, s, p), left), (mRy, at(r, s, p), right)]
            stores.append(put(f"sq{p}", r, (square + left * left) + 36.0 * FLOOR))
        yield stores

    def shift_right(s, r):
        right = mRy[s, 0, rows(r), :]
        yield
        yield [put("right_after", r, shift_lanes(right, -1))]

    def advance(s, r):
        late = (s % 2).astype(jnp.float32)
        keep = 0.5 * late
        take = 1.0 - keep
        before = jnp.maximum(s - 1, 0)
        square = [load(f"sq{p}", r) for p in PARITIES]
        rights = [mRy[s, 1, rows(r), :], load("right_after", r)]
        columns = [mRx[s, p, rows(r, 1), :] for p in PARITIES]
        now = [U[s, p, rows(r), :] for p in PARITIES]
        past = [U[before, p, rows(r), :] for p in PARITIES]
        rates = [rate[p, rows(r), :] for p in PARITIES]
        yield
        stores = []
        for p in PARITIES:
            total = square[p] + (rights[p] * rights[p] + columns[p] * columns[p])
            inverse = lax.rsqrt(total)
            moved = now[p] - rates[p] * (total * inverse)
            stores += [
                (rinv, at(r, s, p), inverse),
                (U, at(r, s + 1, p), keep * past[p] + take * moved),
            ]
        yield stores

    def forward_next(s, r):
        over = r + BLOCK >= forward_end(s)
        last = jnp.logical_and(over, s == STAGES - 1)
        done = r == IDLE
        s_next = jnp.where(over, jnp.minimum(s + 1, STAGES - 1), s)
        r_next = jnp.where(over, forward_start(s_next), r + BLOCK)
        r_next = jnp.where(jnp.logical_or(last, done), IDLE, r_next)
        return s_next, r_next

    forward_count = sum(-(-(forward_end(s) - forward_start(s)) // BLOCK) for s in range(STAGES))

    def forward_step(_, state):
        lag = [(s, aligned(r)) for s, r in state]
        together(
            advance(*lag[6]),
            shift_right(*lag[5]),
            faces(*lag[4]),
            shift_rows(*lag[2]),
            smooth_columns(*lag[2]),
            smooth_rows(*lag[1]),
            differences(*lag[0]),
        )
        return (forward_next(*state[0]),) + state[:6]

    zero = jnp.int32(0)
    idle = jnp.int32(IDLE)
    lax.fori_loop(
        0,
        forward_count + 6,
        forward_step,
        ((zero, jnp.int32(forward_start(0))),) + ((zero, idle),) * 6,
    )

    load, put = tools(BACKWARD_WORK)

    def weigh(s, r):
        loads = []
        for p in PARITIES:
            loads.append((
                g[p, rows(r), :],
                rinv[s, p, rows(r), :],
                rga[p, rows(r), :],
                rate[p, rows(r), :],
                [U[s, p, rows(r, o), :] for o in (-1, 0, 1, 2)],
            ))
        yield
        stores = []
        for p in PARITIES:
            weight, inverse, total, rates, (um, u0, u1, u2) = loads[p]
            m0, m1, m2 = u0 - um, u1 - u0, u2 - u1
            d0, d1 = m1 - m0, m2 - m1
            stores += [
                (rga, at(r, p), total + weight * (1.0 / inverse)),
                put(f"w{p}", r, (rates * weight) * inverse),
                put(f"ex{p}", r, d1 - d0),
                put(f"tx{p}", r, 0.5 * (d0 + d1)),
            ]
        even, odd = loads[0][4][1], loads[1][4][1]
        stores += [
            put("odd_before", r, shift_lanes(odd, 1)),
            put("even_after", r, shift_lanes(even, -1)),
            put("odd_after", r, shift_lanes(odd, -1)),
        ]
        yield stores

    def differ_rows(s, r):
        even, odd = (U[s, p, rows(r), :] for p in PARITIES)
        odd_before, even_after, odd_after = (load(n, r) for n in ("odd_before", "even_after", "odd_after"))
        yield
        m = [even - odd_before, odd - even, even_after - odd, odd_after - even_after]
        d = [b - a for a, b in zip(m[:-1], m[1:])]
        e = [b - a for a, b in zip(d[:-1], d[1:])]
        stores = [put("fc", r, e[0] - e[1])]
        for p in PARITIES:
            stores += [put(f"ey{p}", r, e[p]), put(f"ty{p}", r, 0.5 * (d[p] + d[p + 1]))]
        yield stores

    def shift_before(s, r):
        pairs = (("ey1", "ey1_before"), ("fc", "fa"), ("w1", "w1_before"))
        values = [load(name, r) for name, _ in pairs]
        yield
        yield [put(name, r, shift_lanes(value, 1)) for (_, name), value in zip(pairs, values)]

    def face_adjoints(s, r):
        loads = []
        for p in PARITIES:
            loads.append((
                load(f"w{p}", r), mLx[s, p, rows(r), :],
                load(f"w{p}", r, -1), mRx[s, p, rows(r), :],
                (i1x[s, p, rows(r, -2), :], g2x[s, p, rows(r, -1), :], i3x[s, p, rows(r), :]),
                [load(f"ex{p}", r, o) for o in (-2, -1, 0)],
                mLy[s, p, rows(r), :],
                load("w0" if p == 1 else "w1_before", r), mRy[s, p, rows(r), :],
                (i1y[s, p, rows(r), :], g2y[s, p, rows(r), :], i3y[s, p, rows(r), :]),
            ))
        fa, fc = load("fa", r), load("fc", r)
        ey1_before, ey0 = load("ey1_before", r), load("ey0", r)
        yield
        stores = []
        f = (fa, ey1_before - ey0, fc)
        for p in PARITIES:
            w, leftx, wx, rightx, terms, e, lefty, wy, righty, termsy = loads[p]
            parts = face_adjoint(w * leftx, wx * rightx, *terms, e[0] - e[1], e[1] - e[2])
            stores += [put(f"x{n}_{p}", r, part) for n, part in parts.items()]
            parts = face_adjoint(w * lefty, wy * righty, *termsy, f[p], f[p + 1])
            stores += [put(f"y{n}_{p}", r, part) for n, part in parts.items()]
        yield stores

    def shift_after(s, r):
        values = [load("y" + name, r) for name in AFTER]
        yield
        yield [put("after_" + name, r, shift_lanes(value, -1)) for name, value in zip(AFTER, values)]

    def rows_adjoint(s, r):
        loads = []
        for p in PARITIES:
            ahead = (lambda n: load(f"y{n}_1", r)) if p == 0 else (lambda n: load(f"after_{n}_0", r))
            loads.append((
                load(f"ey{p}", r), load(f"ty{p}", r),
                load(f"after_p1_{p}", r), ahead("g2"), load(f"yp3_{p}", r),
                load(f"after_f1_{p}", r), ahead("h"), load(f"yf2_{p}", r),
                load(f"ybr_{p}", r), ahead("bq"),
            ))
        yield
        stores = []
        for p in PARITIES:
            lower, upper = smoothness_adjoint(*loads[p][:8])
            stores += [put(f"Ry{p}", r, lower + (loads[p][8] + loads[p][9])), put(f"Qy{p}", r, upper)]
        yield stores

    def columns_adjoint(s, r):
        loads = []
        for p in PARITIES:
            loads.append((
                load(f"ex{p}", r), load(f"tx{p}", r),
                load(f"xp1_{p}", r, 2), load(f"xg2_{p}", r, 1), load(f"xp3_{p}", r),
                load(f"xf1_{p}", r, 2), load(f"xh_{p}", r, 1), load(f"xf2_{p}", r),
                load(f"xbr_{p}", r), load(f"xbq_{p}", r, 2),
            ))
        yield
        stores = []
        for p in PARITIES:
            lower, upper = smoothness_adjoint(*loads[p][:8])
            stores += [put(f"Rx{p}", r, lower + loads[p][8]), put(f"Tx{p}", r, upper + loads[p][9])]
        yield stores

    def second_adjoint(s, r):
        columns = [(load(f"Rx{p}", r), load(f"Tx{p}", r, -1)) for p in PARITIES]
        lower = [load(f"Ry{p}", r) for p in PARITIES]
        upper = [load(f"Qy{p}", r) for p in PARITIES]
        yield
        stores = [put(f"Dx{p}", r, columns[p][0] + columns[p][1]) for p in PARITIES]
        stores += [put("Dy0", r, lower[0] + shift_lanes(upper[1], 1)), put("Dy1", r, lower[1] + upper[0])]
        yield stores

    def shift_second(s, r):
        d0, d1 = load("Dy0", r), load("Dy1", r)
        yield
        yield [put("Dy0_after", r, shift_lanes(d0, -1)), put("Dy1_before", r, shift_lanes(d1, 1))]

    def retreat(s, r):
        early = (1 - s % 2).astype(jnp.float32)
        scale = 1.0 - 0.5 * early
        loads = []
        for p in PARITIES:
            loads.append((
                [load(f"Dx{p}", r, o) for o in (-1, 0, 1)],
                [load(n, r) for n in (("Dy1_before", "Dy0", "Dy1") if p == 0 else ("Dy0", "Dy1", "Dy0_after"))],
                load(f"xdA_{p}", r), load(f"xdA_{p}", r, 1),
                load(f"ydA_{p}", r), load("ydA_1" if p == 0 else "after_dA_0", r),
                g[p, rows(r), :],
                held[p, rows(r), :],
            ))
        yield
        stores = []
        for p in PARITIES:
            dx, dy, ax0, ax1, ay0, ay1, old, kept = loads[p]
            back = 6.0 * ((ax0 - ax1) + (ay0 - ay1))
            back = back + ((dx[0] - dx[1]) + (dx[2] - dx[1]))
            back = back + ((dy[0] - dy[1]) + (dy[2] - dy[1]))
            stores += [(g, at(r, p), scale * ((old - back) + early * kept)), (held, at(r, p), old)]
        yield stores

    def backward_next(s, r):
        over = r + BLOCK >= backward_end(s)
        last = jnp.logical_and(over, s == 0)
        done = r == IDLE
        s_next = jnp.where(over, jnp.maximum(s - 1, 0), s)
        r_next = jnp.where(over, backward_start(s_next), r + BLOCK)
        r_next = jnp.where(jnp.logical_or(last, done), IDLE, r_next)
        return s_next, r_next

    backward_count = sum(-(-(backward_end(s) - backward_start(s)) // BLOCK) for s in range(STAGES))

    def backward_step(_, state):
        lag = [(s, aligned(r)) for s, r in state]
        together(
            retreat(*lag[8]),
            shift_second(*lag[7]),
            second_adjoint(*lag[6]),
            columns_adjoint(*lag[5]),
            rows_adjoint(*lag[5]),
            shift_after(*lag[4]),
            face_adjoints(*lag[3]),
            shift_before(*lag[2]),
            differ_rows(*lag[1]),
            weigh(*lag[0]),
        )
        return (backward_next(*state[0]),) + state[:8]

    last = jnp.int32(STAGES - 1)
    lax.fori_loop(
        0,
        backward_count + 8,
        backward_step,
        ((last, jnp.int32(backward_start(STAGES - 1))),) + ((last, idle),) * 8,
    )

    for n in range(3):
        for p in PARITIES:
            if n == 0:
                value = U[STAGES, p, own, :]
            elif n == 1:
                value = (-DT / 6.0) * rga[p, own, :]
            else:
                value = 2.0 * g[p, own, :]
            stage_out[pl.ds(p, 128, stride=2), :] = value.T
        for device in range(16):
            out[device, n] = stage_out[16 * device : 16 * device + 16, :]


def sweep(core, from_left, from_right):
    full = (2, ROWS, 128)
    f32 = jnp.float32
    staged = pltpu.VMEM((STAGES,) + full, f32)
    plain = pltpu.VMEM(full, f32)
    return pl.pallas_call(
        kernel,
        out_shape=pltpu.VMEM((16, 3, 16, 128), f32),
        in_specs=[pl.BlockSpec(memory_space=pltpu.VMEM)] * 3,
        out_specs=pl.BlockSpec(memory_space=pltpu.VMEM),
        scratch_shapes=[pltpu.VMEM((STAGES + 1,) + full, f32)]
        + [staged] * 11
        + [plain] * 4
        + [
            pltpu.VMEM((256, 128), f32),
        ]
        + [pltpu.VMEM((ROWS, 128), f32)] * SLOTS,
        compiler_params=pltpu.CompilerParams(vmem_limit_bytes=61 * 2**20),
    )(core, from_left, from_right)


def turn_kernel(blocks, core, low, high, rows_ref):
    for n in range(3):
        for device in range(16):
            rows_ref[16 * device : 16 * device + 16, :] = blocks[device, n]
        for p in PARITIES:
            core[n, p] = rows_ref[pl.ds(p, 128, stride=2), :].T
    for p in PARITIES:
        for n, (width, start) in enumerate(((HALO, 0), (HALO, HALO), (HALO_COT, 2 * HALO))):
            low[p, start : start + width, :] = core[n, p, 0:width, :]
            high[p, start : start + width, :] = core[n, p, WIDTH - width : WIDTH, :]


def turn(blocks):
    f32 = jnp.float32
    edge = pltpu.VMEM((2, 2 * HALO + HALO_COT, 128), f32)
    return pl.pallas_call(
        turn_kernel,
        out_shape=(pltpu.VMEM((3, 2, 128, 128), f32), edge, edge),
        in_specs=[pl.BlockSpec(memory_space=pltpu.VMEM)],
        out_specs=[pl.BlockSpec(memory_space=pltpu.VMEM)] * 3,
        scratch_shapes=[pltpu.VMEM((256, 128), f32)],
    )(blocks)


CHAIN = (0, 1, 5, 4, 8, 9, 13, 12, 14, 15, 11, 10, 6, 7, 3, 2)


def columns_held(device):
    place = CHAIN.index(device)
    backwards = lax.axis_index("gx") % 2
    strip = place + backwards * (len(CHAIN) - 1 - 2 * place)
    return pl.ds(pl.multiple_of(strip * WIDTH, WIDTH), WIDTH)


def pack_kernel(level_set, spread_rate, cotangent, blocks):
    for device in range(len(CHAIN)):
        columns = columns_held(device)
        for n, ref in enumerate((level_set, spread_rate, cotangent)):
            blocks[device, n] = ref[:, columns]


def unpack_kernel(blocks, final_state, rate_gradient, initial_gradient):
    for device in range(len(CHAIN)):
        columns = columns_held(device)
        for n, ref in enumerate((final_state, rate_gradient, initial_gradient)):
            ref[:, columns] = blocks[device, n]


def near(array):
    return pltpu.with_memory_space_constraint(array, pltpu.VMEM)


def shards(level_set, spread_rate, cotangent):
    bands, runs = lax.axis_size("gy"), lax.axis_size("gx")
    vmem = pl.BlockSpec(memory_space=pltpu.VMEM)
    block = jax.ShapeDtypeStruct(level_set.shape, jnp.float32)
    blocks = pl.pallas_call(
        pack_kernel,
        out_shape=pltpu.VMEM((bands, 3, level_set.shape[0], WIDTH), jnp.float32),
        in_specs=[vmem] * 3,
        out_specs=vmem,
    )(*(pltpu.with_memory_space_constraint(x, pltpu.HBM) for x in (level_set, spread_rate, cotangent)))
    blocks = near(lax.all_to_all(blocks, "gy", 0, 0))
    core, low, high = turn(blocks)
    place = [k * runs + x for x in range(runs) for k in (CHAIN if x % 2 == 0 else CHAIN[::-1])]
    up = list(zip(place, place[1:] + place[:1]))
    from_left = lax.ppermute(high, ("gy", "gx"), up)
    from_right = lax.ppermute(low, ("gy", "gx"), [(b, a) for a, b in up])
    core, from_left, from_right = near(core), near(from_left), near(from_right)
    done = near(lax.all_to_all(sweep(core, from_left, from_right), "gy", 0, 0))
    return pl.pallas_call(
        unpack_kernel,
        out_shape=(block,) * 3,
        in_specs=[vmem],
        out_specs=(vmem,) * 3,
    )(done)


def solution(mesh):
    spec = P("gy", "gx")
    return jax.shard_map(
        shards, mesh=mesh, in_specs=(spec,) * 3, out_specs=(spec,) * 3, check_vma=False
    )
```

```python
import jax
import jax.numpy as jnp
import numpy as np
from jax import lax
from jax.experimental import pallas as pl
from jax.experimental.pallas import tpu as pltpu
from jax.sharding import PartitionSpec as P

STEPS = 6
STAGES = 2 * STEPS
DT = 0.2
EPS = 0.001
FLOOR = 0.25

WIDTH = 128
HALO = 72
HALO_COT = 40
PAD = 16
FORWARD_BLOCK = 24
BACKWARD_BLOCK = 16
TILES = (WIDTH + 2 * HALO) // 8
OWN = PAD + HALO
IDLE = PAD + 2 * HALO + WIDTH + 8
ROWS = IDLE + max(FORWARD_BLOCK, BACKWARD_BLOCK) + 8
PARITIES = (0, 1)

FACE_PARTS = ("p1", "g2", "p3", "f1", "f2", "h", "bq", "br", "dA")
BACKWARD_WORK = (
    ("w0", "w1"),
    ("odd_before", "even_after", "odd_after"),
    ("ex0", "ex1", "tx0", "tx1"),
    ("ey0", "ey1", "ty0", "ty1", "fc"),
    ("ey1_before", "fa", "w1_before"),
    tuple(f"x{n}_{p}" for n in FACE_PARTS for p in PARITIES),
    tuple(f"y{n}_{p}" for n in FACE_PARTS for p in PARITIES),
    ("Rx0", "Rx1", "Tx0", "Tx1"),
    ("Ry0", "Ry1", "Qy0", "Qy1"),
    ("Dx0", "Dx1", "Dy0", "Dy1"),
)
FORWARD_WORK = (
    ("ex0", "ex1"),
    ("odd_before", "even_after", "odd_after"),
    ("mx0", "mx1", "dx0", "dx1"),
    (),
    ("dy1_before", "ey1_before", "fa"),
    ("my0", "my1", "dy0", "dy1", "ey0", "ey1", "i1_0", "i1_1", "g2_1", "fc"),
    (),
    ("sq0", "sq1"),
    (),
    (),
)


class Part:
    def __init__(self, *places):
        self.places = places

    def __getitem__(self, index):
        s, p, *rest = index
        ref, k = self.places[p]
        return ref[(s, k, *rest)]

    def __setitem__(self, index, value):
        s, p, *rest = index
        ref, k = self.places[p]
        ref[(s, k, *rest)] = value


def shift_lanes(value, by):
    return pltpu.roll(value, by % 128, 1)


def smoothness(e, t):
    h = EPS + (13.0 / 12.0 * e) * e
    plus, minus = t + e, t - e
    return h + plus * plus, h + t * t, h + minus * minus


def face_values(m, q, r, i1, g2, i3, f1, f2):
    x, y = g2 * i1, g2 * i3
    x, y = x * x, y * y
    a, b = x * f1, y * f2
    s = a + b
    s = s + s
    total = (x + y) + 6.0
    six = 6.0 * m
    p = q + r
    left = ((six + p) + r) + (s + b) * (1.0 / (total + (y + y)))
    right = ((p - six) + q) + (s + a) * (1.0 / (total + (x + x)))
    return jnp.maximum(left, 0.0), jnp.maximum(right, 0.0)


def face_adjoint(aL, aR, i1, g2, i3, f1, f2):
    x, y = g2 * i1, g2 * i3
    x, y = x * x, y * y
    a, b = x * f1, y * f2
    s = a + b
    s = s + s
    total = (x + y) + 6.0
    kL = 1.0 / (total + (y + y))
    kR = 1.0 / (total + (x + x))
    bL, bR = aL * kL, aR * kR
    cL = bL * ((s + b) * kL)
    cR = bR * ((s + a) * kR)
    both = bL + bR
    both = both + both
    on_a, on_b = both + bR, both + bL
    gX = a * on_a - x * (cL + 3.0 * cR)
    gY = b * on_b - y * (3.0 * cL + cR)
    gf1, gf2 = x * on_a, y * on_b
    aS = aL + aR
    return dict(
        p1=gX * i1, g2=(gX + gY) * (1.0 / g2), p3=gY * i3,
        f1=gf1, f2=gf2, h=gf2 - gf1,
        bq=aS + aR, br=aS + aL, dA=aL - aR,
    )


def smoothness_adjoint(e, t, p1, g2, p3, f1, h, f2):
    v1, v2, v3 = (t + e) * p1, t * g2, (t - e) * p3
    on_e = ((13.0 / 3.0) * e) * (g2 - (p1 + p3)) + 4.0 * (v3 - v1) + ((f1 + h) - f2)
    on_t = 2.0 * (v2 - (v1 + v3))
    return on_t - on_e, on_t + on_e


def forward_range(s):
    edge = 3 * (s + 1) - 2
    return (PAD + edge) // 8 * 8, OWN + WIDTH + HALO - edge


def backward_range(s):
    edge = 39 + 3 * (STAGES - 1 - s)
    return (PAD + edge - 4) // 8 * 8, OWN + WIDTH + HALO - edge + 3


def groups_in_order():
    forward, backward = [(0, IDLE)] * 6, [(STAGES - 1, IDLE)] * 7
    for s in range(STAGES):
        forward += [(s, r) for r in range(*forward_range(s), FORWARD_BLOCK)]
    for s in reversed(range(STAGES)):
        groups = [(s, r) for r in range(*backward_range(s), BACKWARD_BLOCK)]
        backward += groups + [(s, IDLE)] * (9 - len(groups))
    return forward + [(STAGES - 1, IDLE)] * 6, backward + [(0, IDLE)] * 8


def kernel(order, core, from_left, from_right, out, U, SX, SA, SB, SM, rinv, rate, g, held, rga, stage_out, *work):
    i1x, g2x, i3x = (Part((SX, k), (SX, k + 1)) for k in (0, 2, 4))
    mLx, mRx, mLy, mRy = (Part((SM, k), (SM, k + 1)) for k in (0, 2, 4, 6))
    i3y = Part((SA, 0), (SA, 1))
    i1y = Part((SB, 0), (SB, 1))
    g2y = Part((SB, 2), (SA, 2))
    own = slice(OWN, OWN + WIDTH)
    low = slice(PAD, PAD + HALO)
    high = slice(OWN + WIDTH, OWN + WIDTH + HALO)
    held[...] = jnp.zeros_like(held)
    rga[...] = jnp.zeros_like(rga)
    for p in PARITIES:
        U[0, p, own, :] = core[0, p]
        U[0, p, low, :] = from_left[p, 0:HALO, :]
        U[0, p, high, :] = from_right[p, 0:HALO, :]
        rate[p, own, :] = (DT / 6.0) * core[1, p]
        rate[p, low, :] = (DT / 6.0) * from_left[p, HALO : 2 * HALO, :]
        rate[p, high, :] = (DT / 6.0) * from_right[p, HALO : 2 * HALO, :]
        g[p, own, :] = 0.5 * core[2, p]
        g[p, OWN - HALO_COT : OWN, :] = 0.5 * from_left[p, 2 * HALO :, :]
        g[p, OWN + WIDTH : OWN + WIDTH + HALO_COT, :] = 0.5 * from_right[p, 2 * HALO :, :]

    block = FORWARD_BLOCK

    def rows(r, offset=0):
        return pl.ds(r + offset, block)

    def together(*phases):
        for phase in phases:
            next(phase)
        stores = [store for phase in phases for store in next(phase)]
        for ref, index, value in stores:
            ref[index] = value

    def at(r, *lead):
        return lead + (rows(r), slice(None))

    def tools(names):
        slot = {name: (ref, n) for ref, group in zip(work, names) for n, name in enumerate(group)}

        def load(name, r, offset=0):
            ref, n = slot[name]
            return ref[n, rows(r, offset), :]

        def put(name, r, value):
            ref, n = slot[name]
            return (ref, at(r, n), value)

        return load, put

    load, put = tools(FORWARD_WORK)

    def differences(s, r):
        us = [[U[s, p, rows(r, o), :] for o in (-1, 0, 1)] for p in PARITIES]
        yield
        stores = []
        for p in PARITIES:
            um, u0, u1 = us[p]
            m0, m1 = u0 - um, u1 - u0
            stores += [put(f"mx{p}", r, m0), put(f"dx{p}", r, m1 - m0)]
        even, odd = us[0][1], us[1][1]
        stores += [
            put("odd_before", r, shift_lanes(odd, 1)),
            put("even_after", r, shift_lanes(even, -1)),
            put("odd_after", r, shift_lanes(odd, -1)),
        ]
        yield stores

    def smooth_columns(s, r):
        ds = [[load(f"dx{p}", r, o) for o in (0, 1)] for p in PARITIES]
        yield
        stores = []
        for p in PARITIES:
            d0, d1 = ds[p]
            e = d1 - d0
            s1, s2, s3 = smoothness(e, 0.5 * (d0 + d1))
            stores += [
                (i1x, at(r, s, p), 1.0 / s1),
                (g2x, at(r, s, p), s2),
                (i3x, at(r, s, p), 1.0 / s3),
                put(f"ex{p}", r, e),
            ]
        yield stores

    def smooth_rows(s, r):
        even, odd = (U[s, p, rows(r), :] for p in PARITIES)
        odd_before, even_after, odd_after = (load(n, r) for n in ("odd_before", "even_after", "odd_after"))
        yield
        m = [even - odd_before, odd - even, even_after - odd, odd_after - even_after]
        d = [b - a for a, b in zip(m[:-1], m[1:])]
        e = [b - a for a, b in zip(d[:-1], d[1:])]
        terms = [smoothness(e[p], 0.5 * (d[p] + d[p + 1])) for p in PARITIES]
        stores = []
        for p in PARITIES:
            stores += [
                put(f"my{p}", r, m[p]),
                put(f"dy{p}", r, d[p]),
                put(f"ey{p}", r, e[p]),
                put(f"i1_{p}", r, 1.0 / terms[p][0]),
                (i3y, at(r, s, p), 1.0 / terms[p][2]),
            ]
        stores += [(g2y, at(r, s, 1), terms[0][1]), put("g2_1", r, terms[1][1]), put("fc", r, e[0] - e[1])]
        yield stores

    def shift_rows(s, r):
        names = ("i1_0", "i1_1", "g2_1", "dy1", "ey1", "fc")
        values = [load(name, r) for name in names]
        yield
        i10, i11, g21, dy1, ey1, fc = (shift_lanes(value, 1) for value in values)
        yield [
            (i1y, at(r, s, 0), i10),
            (i1y, at(r, s, 1), i11),
            (g2y, at(r, s, 0), g21),
            put("dy1_before", r, dy1),
            put("ey1_before", r, ey1),
            put("fa", r, fc),
        ]

    def faces(s, r):
        columns = []
        for p in PARITIES:
            columns.append((
                load(f"mx{p}", r),
                load(f"dx{p}", r, -1),
                load(f"dx{p}", r),
                i1x[s, p, rows(r, -2), :], g2x[s, p, rows(r, -1), :], i3x[s, p, rows(r), :],
                [load(f"ex{p}", r, o) for o in (-2, -1, 0)],
            ))
        terms = [(i1y[s, p, rows(r), :], g2y[s, p, rows(r), :], i3y[s, p, rows(r), :]) for p in PARITIES]
        my = [load("my0", r), load("my1", r)]
        dy = [load("dy1_before", r), load("dy0", r), load("dy1", r)]
        fa, fc = load("fa", r), load("fc", r)
        ey1_before, ey0 = load("ey1_before", r), load("ey0", r)
        yield
        stores = []
        fb = ey1_before - ey0
        f = (fa, fb, fc)
        for p in PARITIES:
            m, q, rr, i1, g2, i3, e = columns[p]
            left, right = face_values(m, q, rr, i1, g2, i3, e[0] - e[1], e[1] - e[2])
            stores += [(mLx, at(r, s, p), left), (mRx, at(r, s, p), right)]
            square = left * left
            left, right = face_values(my[p], dy[p], dy[p + 1], *terms[p], f[p], f[p + 1])
            stores += [(mLy, at(r, s, p), left), (mRy, at(r, s, p), right)]
            stores.append(put(f"sq{p}", r, (square + left * left) + 36.0 * FLOOR))
        yield stores

    def advance(s, r):
        late = (s % 2).astype(jnp.float32)
        keep = 0.5 * late
        take = 1.0 - keep
        before = jnp.maximum(s - 1, 0)
        square = [load(f"sq{p}", r) for p in PARITIES]
        rights = [mRy[s, 1, rows(r), :], mRy[s, 0, rows(r), :]]
        columns = [mRx[s, p, rows(r, 1), :] for p in PARITIES]
        now = [U[s, p, rows(r), :] for p in PARITIES]
        past = [U[before, p, rows(r), :] for p in PARITIES]
        rates = [rate[p, rows(r), :] for p in PARITIES]
        yield
        rights[1] = shift_lanes(rights[1], -1)
        stores = []
        for p in PARITIES:
            total = square[p] + (rights[p] * rights[p] + columns[p] * columns[p])
            inverse = lax.rsqrt(total)
            moved = now[p] - rates[p] * (total * inverse)
            stores += [
                (rinv, at(r, s, p), inverse),
                (U, at(r, s + 1, p), keep * past[p] + take * moved),
            ]
        yield stores

    forward, backward = groups_in_order()

    def forward_step(n, state):
        lag = [(s, pl.multiple_of(r, 8)) for s, r in state]
        together(
            faces(*lag[4]),
            advance(*lag[6]),
            shift_rows(*lag[2]),
            smooth_columns(*lag[2]),
            smooth_rows(*lag[1]),
            differences(*lag[0]),
        )
        return ((order[0, n + 7], order[1, n + 7]),) + state[:6]

    lax.fori_loop(0, len(forward) - 6, forward_step, tuple((order[0, 6 - k], order[1, 6 - k]) for k in range(7)))

    block = BACKWARD_BLOCK
    load, put = tools(BACKWARD_WORK)

    def weigh(s, r):
        loads = []
        for p in PARITIES:
            loads.append((
                g[p, rows(r), :],
                rinv[s, p, rows(r), :],
                rga[p, rows(r), :],
                rate[p, rows(r), :],
                [U[s, p, rows(r, o), :] for o in (-1, 0, 1, 2)],
            ))
        yield
        stores = []
        for p in PARITIES:
            weight, inverse, total, rates, (um, u0, u1, u2) = loads[p]
            m0, m1, m2 = u0 - um, u1 - u0, u2 - u1
            d0, d1 = m1 - m0, m2 - m1
            stores += [
                (rga, at(r, p), total + weight * (1.0 / inverse)),
                put(f"w{p}", r, (rates * weight) * inverse),
                put(f"ex{p}", r, d1 - d0),
                put(f"tx{p}", r, 0.5 * (d0 + d1)),
            ]
        even, odd = loads[0][4][1], loads[1][4][1]
        stores += [
            put("odd_before", r, shift_lanes(odd, 1)),
            put("even_after", r, shift_lanes(even, -1)),
            put("odd_after", r, shift_lanes(odd, -1)),
        ]
        yield stores

    def differ_rows(s, r):
        even, odd = (U[s, p, rows(r), :] for p in PARITIES)
        odd_before, even_after, odd_after = (load(n, r) for n in ("odd_before", "even_after", "odd_after"))
        yield
        m = [even - odd_before, odd - even, even_after - odd, odd_after - even_after]
        d = [b - a for a, b in zip(m[:-1], m[1:])]
        e = [b - a for a, b in zip(d[:-1], d[1:])]
        stores = [put("fc", r, e[0] - e[1])]
        for p in PARITIES:
            stores += [put(f"ey{p}", r, e[p]), put(f"ty{p}", r, 0.5 * (d[p] + d[p + 1]))]
        yield stores

    def face_adjoints(s, r):
        loads = []
        for p in PARITIES:
            loads.append((
                load(f"w{p}", r), mLx[s, p, rows(r), :],
                load(f"w{p}", r, -1), mRx[s, p, rows(r), :],
                (i1x[s, p, rows(r, -2), :], g2x[s, p, rows(r, -1), :], i3x[s, p, rows(r), :]),
                [load(f"ex{p}", r, o) for o in (-2, -1, 0)],
                mLy[s, p, rows(r), :],
                mRy[s, p, rows(r), :],
                (i1y[s, p, rows(r), :], g2y[s, p, rows(r), :], i3y[s, p, rows(r), :]),
            ))
        fc, ey1, ey0 = load("fc", r), load("ey1", r), load("ey0", r)
        yield
        stores = []
        f = (shift_lanes(fc, 1), shift_lanes(ey1, 1) - ey0, fc)
        before = (shift_lanes(loads[1][0], 1), loads[0][0])
        for p in PARITIES:
            w, leftx, wx, rightx, terms, e, lefty, righty, termsy = loads[p]
            wy = before[p]
            parts = face_adjoint(w * leftx, wx * rightx, *terms, e[0] - e[1], e[1] - e[2])
            stores += [put(f"x{n}_{p}", r, part) for n, part in parts.items()]
            parts = face_adjoint(w * lefty, wy * righty, *termsy, f[p], f[p + 1])
            stores += [put(f"y{n}_{p}", r, part) for n, part in parts.items()]
        yield stores

    def rows_adjoint(s, r):
        loads = [(load(f"ey{p}", r), load(f"ty{p}", r)) for p in PARITIES]
        even, odd = ({n: load(f"y{n}_{p}", r) for n in FACE_PARTS if n != "dA"} for p in PARITIES)
        yield
        after = {n: shift_lanes(even[n], -1) for n in ("g2", "h", "bq", "p1", "f1")}
        beyond = {n: shift_lanes(odd[n], -1) for n in ("p1", "f1")}
        stores = []
        for p, (first, second, third) in enumerate(((even, odd, after), (odd, after, beyond))):
            lower, upper = smoothness_adjoint(
                *loads[p], third["p1"], second["g2"], first["p3"], third["f1"], second["h"], first["f2"]
            )
            stores += [put(f"Ry{p}", r, lower + (first["br"] + second["bq"])), put(f"Qy{p}", r, upper)]
        yield stores

    def columns_adjoint(s, r):
        loads = []
        for p in PARITIES:
            loads.append((
                load(f"ex{p}", r), load(f"tx{p}", r),
                load(f"xp1_{p}", r, 2), load(f"xg2_{p}", r, 1), load(f"xp3_{p}", r),
                load(f"xf1_{p}", r, 2), load(f"xh_{p}", r, 1), load(f"xf2_{p}", r),
                load(f"xbr_{p}", r), load(f"xbq_{p}", r, 2),
            ))
        yield
        stores = []
        for p in PARITIES:
            lower, upper = smoothness_adjoint(*loads[p][:8])
            stores += [put(f"Rx{p}", r, lower + loads[p][8]), put(f"Tx{p}", r, upper + loads[p][9])]
        yield stores

    def second_adjoint(s, r):
        columns = [(load(f"Rx{p}", r), load(f"Tx{p}", r, -1)) for p in PARITIES]
        lower = [load(f"Ry{p}", r) for p in PARITIES]
        upper = [load(f"Qy{p}", r) for p in PARITIES]
        yield
        stores = [put(f"Dx{p}", r, columns[p][0] + columns[p][1]) for p in PARITIES]
        stores += [put("Dy0", r, lower[0] + shift_lanes(upper[1], 1)), put("Dy1", r, lower[1] + upper[0])]
        yield stores

    def retreat(s, r):
        early = (1 - s % 2).astype(jnp.float32)
        scale = 1.0 - 0.5 * early
        loads = []
        for p in PARITIES:
            loads.append((
                [load(f"Dx{p}", r, o) for o in (-1, 0, 1)],
                load(f"Dy{p}", r),
                load(f"xdA_{p}", r), load(f"xdA_{p}", r, 1),
                load(f"ydA_{p}", r),
                g[p, rows(r), :],
                held[p, rows(r), :],
            ))
        yield
        stores = []
        d0, d1 = loads[0][1], loads[1][1]
        a0, a1 = loads[0][4], loads[1][4]
        rows_of = (
            ((shift_lanes(d1, 1), d0, d1), a0, a1),
            ((d0, d1, shift_lanes(d0, -1)), a1, shift_lanes(a0, -1)),
        )
        for p in PARITIES:
            dx, _, ax0, ax1, _, old, kept = loads[p]
            dy, ay0, ay1 = rows_of[p]
            back = 6.0 * ((ax0 - ax1) + (ay0 - ay1))
            back = back + ((dx[0] - dx[1]) + (dx[2] - dx[1]))
            back = back + ((dy[0] - dy[1]) + (dy[2] - dy[1]))
            stores += [(g, at(r, p), scale * ((old - back) + early * kept)), (held, at(r, p), old)]
        yield stores

    def backward_step(n, state):
        lag = [(s, pl.multiple_of(r, 8)) for s, r in state]
        together(
            retreat(*lag[7]),
            second_adjoint(*lag[5]),
            columns_adjoint(*lag[4]),
            rows_adjoint(*lag[3]),
            face_adjoints(*lag[2]),
            differ_rows(*lag[1]),
            weigh(*lag[0]),
        )
        return ((order[0, n + 8], order[1, n + 8]),) + state[:7]

    begin = len(forward)
    lax.fori_loop(
        begin,
        begin + len(backward) - 7,
        backward_step,
        tuple((order[0, begin + 7 - k], order[1, begin + 7 - k]) for k in range(8)),
    )

    for n in range(3):
        for p in PARITIES:
            if n == 0:
                value = U[STAGES, p, own, :]
            elif n == 1:
                value = (-DT / 6.0) * rga[p, own, :]
            else:
                value = 2.0 * g[p, own, :]
            stage_out[pl.ds(p, 128, stride=2), :] = value.T
        for device in range(16):
            out[device, n] = stage_out[16 * device : 16 * device + 16, :]


def sweep(core, from_left, from_right):
    full = (2, ROWS, 128)
    forward, backward = groups_in_order()
    order = jnp.array(np.array(forward + backward, np.int32).T)
    f32 = jnp.float32
    plain = pltpu.VMEM(full, f32)
    return pl.pallas_call(
        kernel,
        out_shape=pltpu.VMEM((16, 3, 16, 128), f32),
        in_specs=[pl.BlockSpec(memory_space=pltpu.SMEM)] + [pl.BlockSpec(memory_space=pltpu.VMEM)] * 3,
        out_specs=pl.BlockSpec(memory_space=pltpu.VMEM),
        scratch_shapes=[pltpu.VMEM((STAGES + 1,) + full, f32)]
        + [pltpu.VMEM((STAGES, n, ROWS, 128), f32) for n in (6, 3, 3, 8, 2)]
        + [plain] * 4
        + [
            pltpu.VMEM((256, 128), f32),
        ]
        + [pltpu.VMEM((len(group), ROWS, 128), f32) for group in BACKWARD_WORK],
        compiler_params=pltpu.CompilerParams(vmem_limit_bytes=61 * 2**20),
    )(order, core, from_left, from_right)


def turn_kernel(blocks, core, low, high, rows_ref):
    for n in range(3):
        for device in range(16):
            rows_ref[16 * device : 16 * device + 16, :] = blocks[device, n]
        for p in PARITIES:
            core[n, p] = rows_ref[pl.ds(p, 128, stride=2), :].T
    for p in PARITIES:
        for n, (width, start) in enumerate(((HALO, 0), (HALO, HALO), (HALO_COT, 2 * HALO))):
            low[p, start : start + width, :] = core[n, p, 0:width, :]
            high[p, start : start + width, :] = core[n, p, WIDTH - width : WIDTH, :]


def turn(blocks):
    f32 = jnp.float32
    edge = pltpu.VMEM((2, 2 * HALO + HALO_COT, 128), f32)
    return pl.pallas_call(
        turn_kernel,
        out_shape=(pltpu.VMEM((3, 2, 128, 128), f32), edge, edge),
        in_specs=[pl.BlockSpec(memory_space=pltpu.VMEM)],
        out_specs=[pl.BlockSpec(memory_space=pltpu.VMEM)] * 3,
        scratch_shapes=[pltpu.VMEM((256, 128), f32)],
    )(blocks)


CHAIN = (0, 1, 5, 4, 8, 9, 13, 12, 14, 15, 11, 10, 6, 7, 3, 2)


def columns_held(device):
    place = CHAIN.index(device)
    backwards = lax.axis_index("gx") % 2
    strip = place + backwards * (len(CHAIN) - 1 - 2 * place)
    return pl.ds(pl.multiple_of(strip * WIDTH, WIDTH), WIDTH)


def pack_kernel(level_set, spread_rate, cotangent, blocks):
    for device in range(len(CHAIN)):
        columns = columns_held(device)
        for n, ref in enumerate((level_set, spread_rate, cotangent)):
            blocks[device, n] = ref[:, columns]


def unpack_kernel(blocks, final_state, rate_gradient, initial_gradient):
    for device in range(len(CHAIN)):
        columns = columns_held(device)
        for n, ref in enumerate((final_state, rate_gradient, initial_gradient)):
            ref[:, columns] = blocks[device, n]


def near(array):
    return pltpu.with_memory_space_constraint(array, pltpu.VMEM)


def shards(level_set, spread_rate, cotangent):
    bands, runs = lax.axis_size("gy"), lax.axis_size("gx")
    vmem = pl.BlockSpec(memory_space=pltpu.VMEM)
    block = jax.ShapeDtypeStruct(level_set.shape, jnp.float32)
    blocks = pl.pallas_call(
        pack_kernel,
        out_shape=pltpu.VMEM((bands, 3, level_set.shape[0], WIDTH), jnp.float32),
        in_specs=[vmem] * 3,
        out_specs=vmem,
    )(*(pltpu.with_memory_space_constraint(x, pltpu.HBM) for x in (level_set, spread_rate, cotangent)))
    blocks = near(lax.all_to_all(blocks, "gy", 0, 0))
    core, low, high = turn(blocks)
    place = [k * runs + x for x in range(runs) for k in (CHAIN if x % 2 == 0 else CHAIN[::-1])]
    up = list(zip(place, place[1:] + place[:1]))
    from_left = lax.ppermute(high, ("gy", "gx"), up)
    from_right = lax.ppermute(low, ("gy", "gx"), [(b, a) for a, b in up])
    core, from_left, from_right = near(core), near(from_left), near(from_right)
    done = near(lax.all_to_all(sweep(core, from_left, from_right), "gy", 0, 0))
    return pl.pallas_call(
        unpack_kernel,
        out_shape=(block,) * 3,
        in_specs=[vmem],
        out_specs=(vmem,) * 3,
    )(done)


def solution(mesh):
    spec = P("gy", "gx")
    return jax.shard_map(
        shards, mesh=mesh, in_specs=(spec,) * 3, out_specs=(spec,) * 3, check_vma=False
    )
```

```python
import jax
import jax.numpy as jnp
from jax import lax
from jax.experimental import pallas as pl
from jax.experimental.pallas import tpu as pltpu
from jax.sharding import PartitionSpec as P

STEPS = 6
STAGES = 2 * STEPS
DT = 0.2
EPS = 0.001
FLOOR = 0.25

WIDTH = 128
HALO = 72
HALO_COT = 40
PAD = 16
FORWARD_BLOCK = 24
BACKWARD_BLOCK = 16
TILES = (WIDTH + 2 * HALO) // 8
OWN = PAD + HALO
IDLE = PAD + 2 * HALO + WIDTH + 8
ROWS = IDLE + max(FORWARD_BLOCK, BACKWARD_BLOCK) + 8
PARITIES = (0, 1)

FACE_PARTS = ("p1", "g2", "p3", "f1", "f2", "h", "bq", "br", "dA")
BACKWARD_WORK = (
    ("w0", "w1"),
    ("odd_before", "even_after", "odd_after"),
    ("ex0", "ex1", "tx0", "tx1"),
    ("ey0", "ey1", "ty0", "ty1", "fc"),
    ("ey1_before", "fa", "w1_before"),
    tuple(f"x{n}_{p}" for n in FACE_PARTS for p in PARITIES),
    tuple(f"y{n}_{p}" for n in FACE_PARTS for p in PARITIES),
    ("Rx0", "Rx1", "Tx0", "Tx1"),
    ("Ry0", "Ry1", "Qy0", "Qy1"),
    ("Dx0", "Dx1", "Dy0", "Dy1"),
)
FORWARD_WORK = (
    ("ex0", "ex1"),
    ("odd_before", "even_after", "odd_after"),
    ("mx0", "mx1", "dx0", "dx1"),
    (),
    ("dy1_before", "ey1_before", "fa"),
    ("my0", "my1", "dy0", "dy1", "ey0", "ey1", "i1_0", "i1_1", "g2_1", "fc"),
    (),
    ("sq0", "sq1"),
    (),
    (),
)


class Part:
    def __init__(self, *places):
        self.places = places

    def __getitem__(self, index):
        s, p, *rest = index
        ref, k = self.places[p]
        return ref[(s, k, *rest)]

    def __setitem__(self, index, value):
        s, p, *rest = index
        ref, k = self.places[p]
        ref[(s, k, *rest)] = value


def shift_lanes(value, by):
    return pltpu.roll(value, by % 128, 1)


def smoothness(e, t):
    h = EPS + (13.0 / 12.0 * e) * e
    plus, minus = t + e, t - e
    return h + plus * plus, h + t * t, h + minus * minus


def face_values(m, q, r, i1, g2, i3, f1, f2):
    x, y = g2 * i1, g2 * i3
    x, y = x * x, y * y
    a, b = x * f1, y * f2
    s = a + b
    s = s + s
    total = (x + y) + 6.0
    six = 6.0 * m
    p = q + r
    left = ((six + p) + r) + (s + b) * (1.0 / (total + (y + y)))
    right = ((p - six) + q) + (s + a) * (1.0 / (total + (x + x)))
    return jnp.maximum(left, 0.0), jnp.maximum(right, 0.0)


def face_adjoint(aL, aR, i1, g2, i3, f1, f2):
    x, y = g2 * i1, g2 * i3
    x, y = x * x, y * y
    a, b = x * f1, y * f2
    s = a + b
    s = s + s
    total = (x + y) + 6.0
    kL = 1.0 / (total + (y + y))
    kR = 1.0 / (total + (x + x))
    bL, bR = aL * kL, aR * kR
    cL = bL * ((s + b) * kL)
    cR = bR * ((s + a) * kR)
    both = bL + bR
    both = both + both
    on_a, on_b = both + bR, both + bL
    gX = a * on_a - x * (cL + 3.0 * cR)
    gY = b * on_b - y * (3.0 * cL + cR)
    gf1, gf2 = x * on_a, y * on_b
    aS = aL + aR
    return dict(
        p1=gX * i1, g2=(gX + gY) * (1.0 / g2), p3=gY * i3,
        f1=gf1, f2=gf2, h=gf2 - gf1,
        bq=aS + aR, br=aS + aL, dA=aL - aR,
    )


def smoothness_adjoint(e, t, p1, g2, p3, f1, h, f2):
    v1, v2, v3 = (t + e) * p1, t * g2, (t - e) * p3
    on_e = ((13.0 / 3.0) * e) * (g2 - (p1 + p3)) + 4.0 * (v3 - v1) + ((f1 + h) - f2)
    on_t = 2.0 * (v2 - (v1 + v3))
    return on_t - on_e, on_t + on_e


def forward_range(s):
    edge = 3 * (s + 1) - 2
    return (PAD + edge) & ~7, OWN + WIDTH + HALO - edge


def reach(a, b):
    return max(a, b) if isinstance(a, int) else jnp.maximum(a, b)


def backward_range(s):
    edge = 39 + 3 * (STAGES - 1 - s)
    low = (PAD + edge - 4) & ~7
    return low, reach(OWN + WIDTH + HALO - edge + 3, low + 9 * BACKWARD_BLOCK)


def forward_next(s, r):
    r = r + FORWARD_BLOCK
    over = r >= forward_range(s)[1]
    s = jnp.where(over, s + 1, s)
    r = jnp.where(over, forward_range(s)[0], r)
    return jnp.minimum(s, STAGES - 1), jnp.where(s == STAGES, IDLE, r)


def backward_next(s, r):
    r = r + BACKWARD_BLOCK
    over = r >= backward_range(s)[1]
    s = jnp.where(over, s - 1, s)
    r = jnp.where(over, backward_range(s)[0], r)
    return jnp.maximum(s, 0), jnp.where(s < 0, IDLE, r)


def count(reach, block):
    return sum(-(-(int(high) - int(low)) // block) for low, high in map(reach, range(STAGES)))


def kernel(core, from_left, from_right, out, U, SX, SA, SB, SM, rinv, rate, g, held, rga, stage_out, *work):
    i1x, g2x, i3x = (Part((SX, k), (SX, k + 1)) for k in (0, 2, 4))
    mLx, mRx, mLy, mRy = (Part((SM, k), (SM, k + 1)) for k in (0, 2, 4, 6))
    i3y = Part((SA, 0), (SA, 1))
    i1y = Part((SB, 0), (SB, 1))
    g2y = Part((SB, 2), (SA, 2))
    own = slice(OWN, OWN + WIDTH)
    low = slice(PAD, PAD + HALO)
    high = slice(OWN + WIDTH, OWN + WIDTH + HALO)
    held[...] = jnp.zeros_like(held)
    rga[...] = jnp.zeros_like(rga)
    for p in PARITIES:
        U[0, p, own, :] = core[0, p]
        U[0, p, low, :] = from_left[p, 0:HALO, :]
        U[0, p, high, :] = from_right[p, 0:HALO, :]
        rate[p, own, :] = (DT / 6.0) * core[1, p]
        rate[p, low, :] = (DT / 6.0) * from_left[p, HALO : 2 * HALO, :]
        rate[p, high, :] = (DT / 6.0) * from_right[p, HALO : 2 * HALO, :]
        g[p, own, :] = 0.5 * core[2, p]
        g[p, OWN - HALO_COT : OWN, :] = 0.5 * from_left[p, 2 * HALO :, :]
        g[p, OWN + WIDTH : OWN + WIDTH + HALO_COT, :] = 0.5 * from_right[p, 2 * HALO :, :]

    block = FORWARD_BLOCK

    def rows(r, offset=0):
        return pl.ds(r + offset, block)

    def together(*phases):
        for phase in phases:
            next(phase)
        stores = [store for phase in phases for store in next(phase)]
        for ref, index, value in stores:
            ref[index] = value

    def at(r, *lead):
        return lead + (rows(r), slice(None))

    def tools(names):
        slot = {name: (ref, n) for ref, group in zip(work, names) for n, name in enumerate(group)}

        def load(name, r, offset=0):
            ref, n = slot[name]
            return ref[n, rows(r, offset), :]

        def put(name, r, value):
            ref, n = slot[name]
            return (ref, at(r, n), value)

        return load, put

    load, put = tools(FORWARD_WORK)

    def differences(s, r):
        us = [[U[s, p, rows(r, o), :] for o in (-1, 0, 1)] for p in PARITIES]
        yield
        stores = []
        for p in PARITIES:
            um, u0, u1 = us[p]
            m0, m1 = u0 - um, u1 - u0
            stores += [put(f"mx{p}", r, m0), put(f"dx{p}", r, m1 - m0)]
        even, odd = us[0][1], us[1][1]
        stores += [
            put("odd_before", r, shift_lanes(odd, 1)),
            put("even_after", r, shift_lanes(even, -1)),
            put("odd_after", r, shift_lanes(odd, -1)),
        ]
        yield stores

    def smooth_columns(s, r):
        ds = [[load(f"dx{p}", r, o) for o in (0, 1)] for p in PARITIES]
        yield
        stores = []
        for p in PARITIES:
            d0, d1 = ds[p]
            e = d1 - d0
            s1, s2, s3 = smoothness(e, 0.5 * (d0 + d1))
            stores += [
                (i1x, at(r, s, p), 1.0 / s1),
                (g2x, at(r, s, p), s2),
                (i3x, at(r, s, p), 1.0 / s3),
                put(f"ex{p}", r, e),
            ]
        yield stores

    def smooth_rows(s, r):
        even, odd = (U[s, p, rows(r), :] for p in PARITIES)
        odd_before, even_after, odd_after = (load(n, r) for n in ("odd_before", "even_after", "odd_after"))
        yield
        m = [even - odd_before, odd - even, even_after - odd, odd_after - even_after]
        d = [b - a for a, b in zip(m[:-1], m[1:])]
        e = [b - a for a, b in zip(d[:-1], d[1:])]
        terms = [smoothness(e[p], 0.5 * (d[p] + d[p + 1])) for p in PARITIES]
        stores = []
        for p in PARITIES:
            stores += [
                put(f"my{p}", r, m[p]),
                put(f"dy{p}", r, d[p]),
                put(f"ey{p}", r, e[p]),
                put(f"i1_{p}", r, 1.0 / terms[p][0]),
                (i3y, at(r, s, p), 1.0 / terms[p][2]),
            ]
        stores += [(g2y, at(r, s, 1), terms[0][1]), put("g2_1", r, terms[1][1]), put("fc", r, e[0] - e[1])]
        yield stores

    def shift_rows(s, r):
        names = ("i1_0", "i1_1", "g2_1", "dy1", "ey1", "fc")
        values = [load(name, r) for name in names]
        yield
        i10, i11, g21, dy1, ey1, fc = (shift_lanes(value, 1) for value in values)
        yield [
            (i1y, at(r, s, 0), i10),
            (i1y, at(r, s, 1), i11),
            (g2y, at(r, s, 0), g21),
            put("dy1_before", r, dy1),
            put("ey1_before", r, ey1),
            put("fa", r, fc),
        ]

    def faces(s, r):
        columns = []
        for p in PARITIES:
            columns.append((
                load(f"mx{p}", r),
                load(f"dx{p}", r, -1),
                load(f"dx{p}", r),
                i1x[s, p, rows(r, -2), :], g2x[s, p, rows(r, -1), :], i3x[s, p, rows(r), :],
                [load(f"ex{p}", r, o) for o in (-2, -1, 0)],
            ))
        terms = [(i1y[s, p, rows(r), :], g2y[s, p, rows(r), :], i3y[s, p, rows(r), :]) for p in PARITIES]
        my = [load("my0", r), load("my1", r)]
        dy = [load("dy1_before", r), load("dy0", r), load("dy1", r)]
        fa, fc = load("fa", r), load("fc", r)
        ey1_before, ey0 = load("ey1_before", r), load("ey0", r)
        yield
        stores = []
        fb = ey1_before - ey0
        f = (fa, fb, fc)
        for p in PARITIES:
            m, q, rr, i1, g2, i3, e = columns[p]
            left, right = face_values(m, q, rr, i1, g2, i3, e[0] - e[1], e[1] - e[2])
            stores += [(mLx, at(r, s, p), left), (mRx, at(r, s, p), right)]
            square = left * left
            left, right = face_values(my[p], dy[p], dy[p + 1], *terms[p], f[p], f[p + 1])
            stores += [(mLy, at(r, s, p), left), (mRy, at(r, s, p), right)]
            stores.append(put(f"sq{p}", r, (square + left * left) + 36.0 * FLOOR))
        yield stores

    def advance(s, r):
        late = (s % 2).astype(jnp.float32)
        keep = 0.5 * late
        take = 1.0 - keep
        before = jnp.maximum(s - 1, 0)
        square = [load(f"sq{p}", r) for p in PARITIES]
        rights = [mRy[s, 1, rows(r), :], mRy[s, 0, rows(r), :]]
        columns = [mRx[s, p, rows(r, 1), :] for p in PARITIES]
        now = [U[s, p, rows(r), :] for p in PARITIES]
        past = [U[before, p, rows(r), :] for p in PARITIES]
        rates = [rate[p, rows(r), :] for p in PARITIES]
        yield
        rights[1] = shift_lanes(rights[1], -1)
        stores = []
        for p in PARITIES:
            total = square[p] + (rights[p] * rights[p] + columns[p] * columns[p])
            inverse = lax.rsqrt(total)
            moved = now[p] - rates[p] * (total * inverse)
            stores += [
                (rinv, at(r, s, p), inverse),
                (U, at(r, s + 1, p), keep * past[p] + take * moved),
            ]
        yield stores

    def forward_step(_, state):
        lag = [(s, pl.multiple_of(r, 8)) for s, r in state]
        together(
            faces(*lag[3]),
            advance(*lag[5]),
            shift_rows(*lag[2]),
            smooth_columns(*lag[2]),
            smooth_rows(*lag[1]),
            differences(*lag[0]),
        )
        return (forward_next(*state[0]),) + state[:5]

    def at_rest(s, low):
        return (jnp.int32(s), jnp.int32(low))

    lax.fori_loop(
        0,
        count(forward_range, FORWARD_BLOCK) + 5,
        forward_step,
        (at_rest(0, forward_range(0)[0]),) + (at_rest(0, IDLE),) * 5,
    )

    block = BACKWARD_BLOCK
    load, put = tools(BACKWARD_WORK)

    def weigh(s, r):
        loads = []
        for p in PARITIES:
            loads.append((
                g[p, rows(r), :],
                rinv[s, p, rows(r), :],
                rga[p, rows(r), :],
                rate[p, rows(r), :],
                [U[s, p, rows(r, o), :] for o in (-1, 0, 1, 2)],
            ))
        yield
        stores = []
        for p in PARITIES:
            weight, inverse, total, rates, (um, u0, u1, u2) = loads[p]
            m0, m1, m2 = u0 - um, u1 - u0, u2 - u1
            d0, d1 = m1 - m0, m2 - m1
            stores += [
                (rga, at(r, p), total + weight * (1.0 / inverse)),
                put(f"w{p}", r, (rates * weight) * inverse),
                put(f"ex{p}", r, d1 - d0),
                put(f"tx{p}", r, 0.5 * (d0 + d1)),
            ]
        even, odd = loads[0][4][1], loads[1][4][1]
        stores += [
            put("odd_before", r, shift_lanes(odd, 1)),
            put("even_after", r, shift_lanes(even, -1)),
            put("odd_after", r, shift_lanes(odd, -1)),
        ]
        yield stores

    def differ_rows(s, r):
        even, odd = (U[s, p, rows(r), :] for p in PARITIES)
        odd_before, even_after, odd_after = (load(n, r) for n in ("odd_before", "even_after", "odd_after"))
        yield
        m = [even - odd_before, odd - even, even_after - odd, odd_after - even_after]
        d = [b - a for a, b in zip(m[:-1], m[1:])]
        e = [b - a for a, b in zip(d[:-1], d[1:])]
        stores = [put("fc", r, e[0] - e[1])]
        for p in PARITIES:
            stores += [put(f"ey{p}", r, e[p]), put(f"ty{p}", r, 0.5 * (d[p] + d[p + 1]))]
        yield stores

    def face_adjoints(s, r):
        loads = []
        for p in PARITIES:
            loads.append((
                load(f"w{p}", r), mLx[s, p, rows(r), :],
                load(f"w{p}", r, -1), mRx[s, p, rows(r), :],
                (i1x[s, p, rows(r, -2), :], g2x[s, p, rows(r, -1), :], i3x[s, p, rows(r), :]),
                [load(f"ex{p}", r, o) for o in (-2, -1, 0)],
                mLy[s, p, rows(r), :],
                mRy[s, p, rows(r), :],
                (i1y[s, p, rows(r), :], g2y[s, p, rows(r), :], i3y[s, p, rows(r), :]),
            ))
        fc, ey1, ey0 = load("fc", r), load("ey1", r), load("ey0", r)
        yield
        stores = []
        f = (shift_lanes(fc, 1), shift_lanes(ey1, 1) - ey0, fc)
        before = (shift_lanes(loads[1][0], 1), loads[0][0])
        for p in PARITIES:
            w, leftx, wx, rightx, terms, e, lefty, righty, termsy = loads[p]
            wy = before[p]
            parts = face_adjoint(w * leftx, wx * rightx, *terms, e[0] - e[1], e[1] - e[2])
            stores += [put(f"x{n}_{p}", r, part) for n, part in parts.items()]
            parts = face_adjoint(w * lefty, wy * righty, *termsy, f[p], f[p + 1])
            stores += [put(f"y{n}_{p}", r, part) for n, part in parts.items()]
        yield stores

    def rows_adjoint(s, r):
        loads = [(load(f"ey{p}", r), load(f"ty{p}", r)) for p in PARITIES]
        even, odd = ({n: load(f"y{n}_{p}", r) for n in FACE_PARTS if n != "dA"} for p in PARITIES)
        yield
        after = {n: shift_lanes(even[n], -1) for n in ("g2", "h", "bq", "p1", "f1")}
        beyond = {n: shift_lanes(odd[n], -1) for n in ("p1", "f1")}
        stores = []
        for p, (first, second, third) in enumerate(((even, odd, after), (odd, after, beyond))):
            lower, upper = smoothness_adjoint(
                *loads[p], third["p1"], second["g2"], first["p3"], third["f1"], second["h"], first["f2"]
            )
            stores += [put(f"Ry{p}", r, lower + (first["br"] + second["bq"])), put(f"Qy{p}", r, upper)]
        yield stores

    def columns_adjoint(s, r):
        loads = []
        for p in PARITIES:
            loads.append((
                load(f"ex{p}", r), load(f"tx{p}", r),
                load(f"xp1_{p}", r, 2), load(f"xg2_{p}", r, 1), load(f"xp3_{p}", r),
                load(f"xf1_{p}", r, 2), load(f"xh_{p}", r, 1), load(f"xf2_{p}", r),
                load(f"xbr_{p}", r), load(f"xbq_{p}", r, 2),
            ))
        yield
        stores = []
        for p in PARITIES:
            lower, upper = smoothness_adjoint(*loads[p][:8])
            stores += [put(f"Rx{p}", r, lower + loads[p][8]), put(f"Tx{p}", r, upper + loads[p][9])]
        yield stores

    def second_adjoint(s, r):
        columns = [(load(f"Rx{p}", r), load(f"Tx{p}", r, -1)) for p in PARITIES]
        lower = [load(f"Ry{p}", r) for p in PARITIES]
        upper = [load(f"Qy{p}", r) for p in PARITIES]
        yield
        stores = [put(f"Dx{p}", r, columns[p][0] + columns[p][1]) for p in PARITIES]
        stores += [put("Dy0", r, lower[0] + shift_lanes(upper[1], 1)), put("Dy1", r, lower[1] + upper[0])]
        yield stores

    def retreat(s, r):
        early = (1 - s % 2).astype(jnp.float32)
        scale = 1.0 - 0.5 * early
        loads = []
        for p in PARITIES:
            loads.append((
                [load(f"Dx{p}", r, o) for o in (-1, 0, 1)],
                load(f"Dy{p}", r),
                load(f"xdA_{p}", r), load(f"xdA_{p}", r, 1),
                load(f"ydA_{p}", r),
                g[p, rows(r), :],
                held[p, rows(r), :],
            ))
        yield
        stores = []
        d0, d1 = loads[0][1], loads[1][1]
        a0, a1 = loads[0][4], loads[1][4]
        rows_of = (
            ((shift_lanes(d1, 1), d0, d1), a0, a1),
            ((d0, d1, shift_lanes(d0, -1)), a1, shift_lanes(a0, -1)),
        )
        for p in PARITIES:
            dx, _, ax0, ax1, _, old, kept = loads[p]
            dy, ay0, ay1 = rows_of[p]
            back = 6.0 * ((ax0 - ax1) + (ay0 - ay1))
            back = back + ((dx[0] - dx[1]) + (dx[2] - dx[1]))
            back = back + ((dy[0] - dy[1]) + (dy[2] - dy[1]))
            stores += [(g, at(r, p), scale * ((old - back) + early * kept)), (held, at(r, p), old)]
        yield stores

    def backward_step(_, state):
        lag = [(s, pl.multiple_of(r, 8)) for s, r in state]
        together(
            retreat(*lag[7]),
            second_adjoint(*lag[5]),
            columns_adjoint(*lag[4]),
            rows_adjoint(*lag[3]),
            face_adjoints(*lag[2]),
            differ_rows(*lag[1]),
            weigh(*lag[0]),
        )
        return (backward_next(*state[0]),) + state[:7]

    final = STAGES - 1
    lax.fori_loop(
        0,
        count(backward_range, BACKWARD_BLOCK) + 7,
        backward_step,
        (at_rest(final, backward_range(final)[0]),) + (at_rest(final, IDLE),) * 7,
    )

    for n in range(3):
        for p in PARITIES:
            if n == 0:
                value = U[STAGES, p, own, :]
            elif n == 1:
                value = (-DT / 6.0) * rga[p, own, :]
            else:
                value = 2.0 * g[p, own, :]
            stage_out[pl.ds(p, 128, stride=2), :] = value.T
        for device in range(16):
            out[device, n] = stage_out[16 * device : 16 * device + 16, :]


def sweep(core, from_left, from_right):
    full = (2, ROWS, 128)
    f32 = jnp.float32
    plain = pltpu.VMEM(full, f32)
    return pl.pallas_call(
        kernel,
        out_shape=pltpu.VMEM((16, 3, 16, 128), f32),
        in_specs=[pl.BlockSpec(memory_space=pltpu.VMEM)] * 3,
        out_specs=pl.BlockSpec(memory_space=pltpu.VMEM),
        scratch_shapes=[pltpu.VMEM((STAGES + 1,) + full, f32)]
        + [pltpu.VMEM((STAGES, n, ROWS, 128), f32) for n in (6, 3, 3, 8, 2)]
        + [plain] * 4
        + [
            pltpu.VMEM((256, 128), f32),
        ]
        + [pltpu.VMEM((len(group), ROWS, 128), f32) for group in BACKWARD_WORK],
        compiler_params=pltpu.CompilerParams(vmem_limit_bytes=61 * 2**20),
    )(core, from_left, from_right)


def turn_kernel(blocks, core, low, high, rows_ref):
    for n in range(3):
        for device in range(16):
            rows_ref[16 * device : 16 * device + 16, :] = blocks[device, n]
        for p in PARITIES:
            core[n, p] = rows_ref[pl.ds(p, 128, stride=2), :].T
    for p in PARITIES:
        for n, (width, start) in enumerate(((HALO, 0), (HALO, HALO), (HALO_COT, 2 * HALO))):
            low[p, start : start + width, :] = core[n, p, 0:width, :]
            high[p, start : start + width, :] = core[n, p, WIDTH - width : WIDTH, :]


def turn(blocks):
    f32 = jnp.float32
    edge = pltpu.VMEM((2, 2 * HALO + HALO_COT, 128), f32)
    return pl.pallas_call(
        turn_kernel,
        out_shape=(pltpu.VMEM((3, 2, 128, 128), f32), edge, edge),
        in_specs=[pl.BlockSpec(memory_space=pltpu.VMEM)],
        out_specs=[pl.BlockSpec(memory_space=pltpu.VMEM)] * 3,
        scratch_shapes=[pltpu.VMEM((256, 128), f32)],
    )(blocks)


CHAIN = (0, 1, 5, 4, 8, 9, 13, 12, 14, 15, 11, 10, 6, 7, 3, 2)


def columns_held(device):
    place = CHAIN.index(device)
    backwards = lax.axis_index("gx") % 2
    strip = place + backwards * (len(CHAIN) - 1 - 2 * place)
    return pl.ds(pl.multiple_of(strip * WIDTH, WIDTH), WIDTH)


def pack_kernel(level_set, spread_rate, cotangent, blocks):
    for device in range(len(CHAIN)):
        columns = columns_held(device)
        for n, ref in enumerate((level_set, spread_rate, cotangent)):
            blocks[device, n] = ref[:, columns]


def unpack_kernel(blocks, final_state, rate_gradient, initial_gradient):
    for device in range(len(CHAIN)):
        columns = columns_held(device)
        for n, ref in enumerate((final_state, rate_gradient, initial_gradient)):
            ref[:, columns] = blocks[device, n]


def near(array):
    return pltpu.with_memory_space_constraint(array, pltpu.VMEM)


def shards(level_set, spread_rate, cotangent):
    bands, runs = lax.axis_size("gy"), lax.axis_size("gx")
    vmem = pl.BlockSpec(memory_space=pltpu.VMEM)
    block = jax.ShapeDtypeStruct(level_set.shape, jnp.float32)
    blocks = pl.pallas_call(
        pack_kernel,
        out_shape=pltpu.VMEM((bands, 3, level_set.shape[0], WIDTH), jnp.float32),
        in_specs=[vmem] * 3,
        out_specs=vmem,
    )(*(pltpu.with_memory_space_constraint(x, pltpu.HBM) for x in (level_set, spread_rate, cotangent)))
    blocks = near(lax.all_to_all(blocks, "gy", 0, 0))
    core, low, high = turn(blocks)
    place = [k * runs + x for x in range(runs) for k in (CHAIN if x % 2 == 0 else CHAIN[::-1])]
    up = list(zip(place, place[1:] + place[:1]))
    from_left = lax.ppermute(high, ("gy", "gx"), up)
    from_right = lax.ppermute(low, ("gy", "gx"), [(b, a) for a, b in up])
    core, from_left, from_right = near(core), near(from_left), near(from_right)
    done = near(lax.all_to_all(sweep(core, from_left, from_right), "gy", 0, 0))
    return pl.pallas_call(
        unpack_kernel,
        out_shape=(block,) * 3,
        in_specs=[vmem],
        out_specs=(vmem,) * 3,
    )(done)


def solution(mesh):
    spec = P("gy", "gx")
    return jax.shard_map(
        shards, mesh=mesh, in_specs=(spec,) * 3, out_specs=(spec,) * 3, check_vma=False
    )
```

```python
import jax
import jax.numpy as jnp
from jax import lax
from jax.experimental import pallas as pl
from jax.experimental.pallas import tpu as pltpu
from jax.sharding import PartitionSpec as P

STEPS = 6
STAGES = 2 * STEPS
DT = 0.2
EPS = 0.001
FLOOR = 0.25

WIDTH = 128
HALO = 72
HALO_COT = 40
PAD = 16
FORWARD_BLOCK = 24
BACKWARD_BLOCK = 16
TILES = (WIDTH + 2 * HALO) // 8
OWN = PAD + HALO
IDLE = PAD + 2 * HALO + WIDTH + 8
ROWS = IDLE + max(FORWARD_BLOCK, BACKWARD_BLOCK) + 8
PARITIES = (0, 1)

FACE_PARTS = ("p1", "g2", "p3", "f1", "f2", "h", "bq", "br", "dA")
BACKWARD_WORK = (
    ("w0", "w1"),
    ("odd_before", "even_after", "odd_after"),
    ("ex0", "ex1", "tx0", "tx1"),
    ("ey0", "ey1", "ty0", "ty1", "fc"),
    ("ey1_before", "fa", "w1_before"),
    tuple(f"x{n}_{p}" for n in FACE_PARTS for p in PARITIES),
    tuple(f"y{n}_{p}" for n in FACE_PARTS for p in PARITIES),
    ("Rx0", "Rx1", "Tx0", "Tx1"),
    ("Ry0", "Ry1", "Qy0", "Qy1"),
    ("Dx0", "Dx1", "Dy0", "Dy1"),
)
FORWARD_WORK = (
    ("ex0", "ex1"),
    ("odd_before", "even_after", "odd_after"),
    ("mx0", "mx1", "dx0", "dx1"),
    (),
    ("dy1_before", "ey1_before", "fa"),
    ("my0", "my1", "dy0", "dy1", "ey0", "ey1", "i1_0", "i1_1", "g2_1", "fc"),
    (),
    ("sq0", "sq1"),
    (),
    (),
)


class Part:
    def __init__(self, *places):
        self.places = places

    def __getitem__(self, index):
        s, p, *rest = index
        ref, k = self.places[p]
        return ref[(s, k, *rest)]

    def __setitem__(self, index, value):
        s, p, *rest = index
        ref, k = self.places[p]
        ref[(s, k, *rest)] = value


def shift_lanes(value, by):
    return pltpu.roll(value, by % 128, 1)


def smoothness(e, t):
    h = EPS + (13.0 / 12.0 * e) * e
    plus, minus = t + e, t - e
    return h + plus * plus, h + t * t, h + minus * minus


def face_values(m, q, r, i1, g2, i3, f1, f2):
    x, y = g2 * i1, g2 * i3
    x, y = x * x, y * y
    a, b = x * f1, y * f2
    s = a + b
    s = s + s
    total = (x + y) + 6.0
    six = 6.0 * m
    p = q + r
    left = ((six + p) + r) + (s + b) * (1.0 / (total + (y + y)))
    right = ((p - six) + q) + (s + a) * (1.0 / (total + (x + x)))
    return jnp.maximum(left, 0.0), jnp.maximum(right, 0.0)


def face_adjoint(aL, aR, i1, g2, i3, f1, f2):
    x, y = g2 * i1, g2 * i3
    x, y = x * x, y * y
    a, b = x * f1, y * f2
    s = a + b
    s = s + s
    total = (x + y) + 6.0
    kL = 1.0 / (total + (y + y))
    kR = 1.0 / (total + (x + x))
    bL, bR = aL * kL, aR * kR
    cL = bL * ((s + b) * kL)
    cR = bR * ((s + a) * kR)
    both = bL + bR
    both = both + both
    on_a, on_b = both + bR, both + bL
    gX = a * on_a - x * (cL + 3.0 * cR)
    gY = b * on_b - y * (3.0 * cL + cR)
    gf1, gf2 = x * on_a, y * on_b
    aS = aL + aR
    return dict(
        p1=gX * i1, g2=(gX + gY) * (1.0 / g2), p3=gY * i3,
        f1=gf1, f2=gf2, h=gf2 - gf1,
        bq=aS + aR, br=aS + aL, dA=aL - aR,
    )


def smoothness_adjoint(e, t, p1, g2, p3, f1, h, f2):
    v1, v2, v3 = (t + e) * p1, t * g2, (t - e) * p3
    on_e = ((13.0 / 3.0) * e) * (g2 - (p1 + p3)) + 4.0 * (v3 - v1) + ((f1 + h) - f2)
    on_t = 2.0 * (v2 - (v1 + v3))
    return on_t - on_e, on_t + on_e


def forward_range(s):
    edge = 3 * (s + 1) - 2
    return (PAD + edge) & ~7, OWN + WIDTH + HALO - edge


def reach(a, b):
    return max(a, b) if isinstance(a, int) else jnp.maximum(a, b)


def backward_range(s):
    edge = 39 + 3 * (STAGES - 1 - s)
    low = (PAD + edge - 4) & ~7
    return low, reach(OWN + WIDTH + HALO - edge + 3, low + 9 * BACKWARD_BLOCK)


def forward_next(s, r):
    r = r + FORWARD_BLOCK
    over = r >= forward_range(s)[1]
    s = jnp.where(over, s + 1, s)
    r = jnp.where(over, forward_range(s)[0], r)
    return jnp.minimum(s, STAGES - 1), jnp.where(s == STAGES, IDLE, r)


def backward_next(s, r):
    r = r + BACKWARD_BLOCK
    over = r >= backward_range(s)[1]
    s = jnp.where(over, s - 1, s)
    r = jnp.where(over, backward_range(s)[0], r)
    return jnp.maximum(s, 0), jnp.where(s < 0, IDLE, r)


def count(reach, block):
    return sum(-(-(int(high) - int(low)) // block) for low, high in map(reach, range(STAGES)))


def kernel(core, from_left, from_right, out, U, SX, SA, SB, SM, rinv, rate, g, held, rga, stage_out, *work):
    i1x, g2x, i3x = (Part((SX, k), (SX, k + 1)) for k in (0, 2, 4))
    mLx, mRx, mLy, mRy = (Part((SM, k), (SM, k + 1)) for k in (0, 2, 4, 6))
    i3y = Part((SA, 0), (SA, 1))
    i1y = Part((SB, 0), (SB, 1))
    g2y = Part((SB, 2), (SA, 2))
    own = slice(OWN, OWN + WIDTH)
    low = slice(PAD, PAD + HALO)
    high = slice(OWN + WIDTH, OWN + WIDTH + HALO)
    held[...] = jnp.zeros_like(held)
    rga[...] = jnp.zeros_like(rga)
    for p in PARITIES:
        U[0, p, own, :] = core[0, p]
        U[0, p, low, :] = from_left[p, 0:HALO, :]
        U[0, p, high, :] = from_right[p, 0:HALO, :]
        rate[p, own, :] = (DT / 6.0) * core[1, p]
        rate[p, low, :] = (DT / 6.0) * from_left[p, HALO : 2 * HALO, :]
        rate[p, high, :] = (DT / 6.0) * from_right[p, HALO : 2 * HALO, :]
        g[p, own, :] = 0.5 * core[2, p]
        g[p, OWN - HALO_COT : OWN, :] = 0.5 * from_left[p, 2 * HALO :, :]
        g[p, OWN + WIDTH : OWN + WIDTH + HALO_COT, :] = 0.5 * from_right[p, 2 * HALO :, :]

    block = FORWARD_BLOCK

    def rows(r, offset=0):
        return pl.ds(r + offset, block)

    def together(*phases):
        for phase in phases:
            next(phase)
        stores = [store for phase in phases for store in next(phase)]
        for ref, index, value in stores:
            ref[index] = value

    def at(r, *lead):
        return lead + (rows(r), slice(None))

    def tools(names):
        slot = {name: (ref, n) for ref, group in zip(work, names) for n, name in enumerate(group)}

        def load(name, r, offset=0):
            ref, n = slot[name]
            return ref[n, rows(r, offset), :]

        def put(name, r, value):
            ref, n = slot[name]
            return (ref, at(r, n), value)

        return load, put

    load, put = tools(FORWARD_WORK)

    def differences(s, r):
        us = [[U[s, p, rows(r, o), :] for o in (-1, 0, 1)] for p in PARITIES]
        yield
        stores = []
        for p in PARITIES:
            um, u0, u1 = us[p]
            m0, m1 = u0 - um, u1 - u0
            stores += [put(f"mx{p}", r, m0), put(f"dx{p}", r, m1 - m0)]
        even, odd = us[0][1], us[1][1]
        stores += [
            put("odd_before", r, shift_lanes(odd, 1)),
            put("even_after", r, shift_lanes(even, -1)),
            put("odd_after", r, shift_lanes(odd, -1)),
        ]
        yield stores

    def smooth_columns(s, r):
        ds = [[load(f"dx{p}", r, o) for o in (0, 1)] for p in PARITIES]
        yield
        stores = []
        for p in PARITIES:
            d0, d1 = ds[p]
            e = d1 - d0
            s1, s2, s3 = smoothness(e, 0.5 * (d0 + d1))
            stores += [
                (i1x, at(r, s, p), 1.0 / s1),
                (g2x, at(r, s, p), s2),
                (i3x, at(r, s, p), 1.0 / s3),
                put(f"ex{p}", r, e),
            ]
        yield stores

    def smooth_rows(s, r):
        even, odd = (U[s, p, rows(r), :] for p in PARITIES)
        odd_before, even_after, odd_after = (load(n, r) for n in ("odd_before", "even_after", "odd_after"))
        yield
        m = [even - odd_before, odd - even, even_after - odd, odd_after - even_after]
        d = [b - a for a, b in zip(m[:-1], m[1:])]
        e = [b - a for a, b in zip(d[:-1], d[1:])]
        terms = [smoothness(e[p], 0.5 * (d[p] + d[p + 1])) for p in PARITIES]
        stores = []
        for p in PARITIES:
            stores += [
                put(f"my{p}", r, m[p]),
                put(f"dy{p}", r, d[p]),
                put(f"ey{p}", r, e[p]),
                put(f"i1_{p}", r, 1.0 / terms[p][0]),
                (i3y, at(r, s, p), 1.0 / terms[p][2]),
            ]
        stores += [(g2y, at(r, s, 1), terms[0][1]), put("g2_1", r, terms[1][1]), put("fc", r, e[0] - e[1])]
        yield stores

    def shift_rows(s, r):
        names = ("i1_0", "i1_1", "g2_1", "dy1", "ey1", "fc")
        values = [load(name, r) for name in names]
        yield
        i10, i11, g21, dy1, ey1, fc = (shift_lanes(value, 1) for value in values)
        yield [
            (i1y, at(r, s, 0), i10),
            (i1y, at(r, s, 1), i11),
            (g2y, at(r, s, 0), g21),
            put("dy1_before", r, dy1),
            put("ey1_before", r, ey1),
            put("fa", r, fc),
        ]

    def faces(s, r):
        columns = []
        for p in PARITIES:
            columns.append((
                load(f"mx{p}", r),
                load(f"dx{p}", r, -1),
                load(f"dx{p}", r),
                i1x[s, p, rows(r, -2), :], g2x[s, p, rows(r, -1), :], i3x[s, p, rows(r), :],
                [load(f"ex{p}", r, o) for o in (-2, -1, 0)],
            ))
        terms = [(i1y[s, p, rows(r), :], g2y[s, p, rows(r), :], i3y[s, p, rows(r), :]) for p in PARITIES]
        my = [load("my0", r), load("my1", r)]
        dy = [load("dy1_before", r), load("dy0", r), load("dy1", r)]
        fa, fc = load("fa", r), load("fc", r)
        ey1_before, ey0 = load("ey1_before", r), load("ey0", r)
        yield
        stores = []
        fb = ey1_before - ey0
        f = (fa, fb, fc)
        for p in PARITIES:
            m, q, rr, i1, g2, i3, e = columns[p]
            left, right = face_values(m, q, rr, i1, g2, i3, e[0] - e[1], e[1] - e[2])
            stores += [(mLx, at(r, s, p), left), (mRx, at(r, s, p), right)]
            square = left * left
            left, right = face_values(my[p], dy[p], dy[p + 1], *terms[p], f[p], f[p + 1])
            stores += [(mLy, at(r, s, p), left), (mRy, at(r, s, p), right)]
            stores.append(put(f"sq{p}", r, (square + left * left) + 36.0 * FLOOR))
        yield stores

    def advance(s, r):
        late = (s % 2).astype(jnp.float32)
        keep = 0.5 * late
        take = 1.0 - keep
        before = jnp.maximum(s - 1, 0)
        square = [load(f"sq{p}", r) for p in PARITIES]
        rights = [mRy[s, 1, rows(r), :], mRy[s, 0, rows(r), :]]
        columns = [mRx[s, p, rows(r, 1), :] for p in PARITIES]
        now = [U[s, p, rows(r), :] for p in PARITIES]
        past = [U[before, p, rows(r), :] for p in PARITIES]
        rates = [rate[p, rows(r), :] for p in PARITIES]
        yield
        rights[1] = shift_lanes(rights[1], -1)
        stores = []
        for p in PARITIES:
            total = square[p] + (rights[p] * rights[p] + columns[p] * columns[p])
            inverse = lax.rsqrt(total)
            moved = now[p] - rates[p] * (total * inverse)
            stores += [
                (rinv, at(r, s, p), inverse),
                (U, at(r, s + 1, p), keep * past[p] + take * moved),
            ]
        yield stores

    def forward_step(_, state):
        lag = [(s, pl.multiple_of(r, 8)) for s, r in state]
        together(
            faces(*lag[3]),
            advance(*lag[5]),
            shift_rows(*lag[2]),
            smooth_columns(*lag[2]),
            smooth_rows(*lag[1]),
            differences(*lag[0]),
        )
        return (forward_next(*state[0]),) + state[:5]

    def at_rest(s, low):
        return (jnp.int32(s), jnp.int32(low))

    lax.fori_loop(
        0,
        count(forward_range, FORWARD_BLOCK) + 5,
        forward_step,
        (at_rest(0, forward_range(0)[0]),) + (at_rest(0, IDLE),) * 5,
    )

    block = BACKWARD_BLOCK
    load, put = tools(BACKWARD_WORK)

    def weigh(s, r):
        loads = []
        for p in PARITIES:
            loads.append((
                g[p, rows(r), :],
                rinv[s, p, rows(r), :],
                rga[p, rows(r), :],
                rate[p, rows(r), :],
                [U[s, p, rows(r, o), :] for o in (-1, 0, 1, 2)],
            ))
        yield
        stores = []
        for p in PARITIES:
            weight, inverse, total, rates, (um, u0, u1, u2) = loads[p]
            m0, m1, m2 = u0 - um, u1 - u0, u2 - u1
            d0, d1 = m1 - m0, m2 - m1
            stores += [
                (rga, at(r, p), total + weight * (1.0 / inverse)),
                put(f"w{p}", r, (rates * weight) * inverse),
                put(f"ex{p}", r, d1 - d0),
                put(f"tx{p}", r, 0.5 * (d0 + d1)),
            ]
        even, odd = loads[0][4][1], loads[1][4][1]
        stores += [
            put("odd_before", r, shift_lanes(odd, 1)),
            put("even_after", r, shift_lanes(even, -1)),
            put("odd_after", r, shift_lanes(odd, -1)),
        ]
        yield stores

    def differ_rows(s, r):
        even, odd = (U[s, p, rows(r), :] for p in PARITIES)
        odd_before, even_after, odd_after = (load(n, r) for n in ("odd_before", "even_after", "odd_after"))
        yield
        m = [even - odd_before, odd - even, even_after - odd, odd_after - even_after]
        d = [b - a for a, b in zip(m[:-1], m[1:])]
        e = [b - a for a, b in zip(d[:-1], d[1:])]
        stores = [put("fc", r, e[0] - e[1])]
        for p in PARITIES:
            stores += [put(f"ey{p}", r, e[p]), put(f"ty{p}", r, 0.5 * (d[p] + d[p + 1]))]
        yield stores

    def face_adjoints(s, r):
        loads = []
        for p in PARITIES:
            loads.append((
                load(f"w{p}", r), mLx[s, p, rows(r), :],
                load(f"w{p}", r, -1), mRx[s, p, rows(r), :],
                (i1x[s, p, rows(r, -2), :], g2x[s, p, rows(r, -1), :], i3x[s, p, rows(r), :]),
                [load(f"ex{p}", r, o) for o in (-2, -1, 0)],
                mLy[s, p, rows(r), :],
                mRy[s, p, rows(r), :],
                (i1y[s, p, rows(r), :], g2y[s, p, rows(r), :], i3y[s, p, rows(r), :]),
            ))
        fc, ey1, ey0 = load("fc", r), load("ey1", r), load("ey0", r)
        yield
        stores = []
        f = (shift_lanes(fc, 1), shift_lanes(ey1, 1) - ey0, fc)
        before = (shift_lanes(loads[1][0], 1), loads[0][0])
        for p in PARITIES:
            w, leftx, wx, rightx, terms, e, lefty, righty, termsy = loads[p]
            wy = before[p]
            parts = face_adjoint(w * leftx, wx * rightx, *terms, e[0] - e[1], e[1] - e[2])
            stores += [put(f"x{n}_{p}", r, part) for n, part in parts.items()]
            parts = face_adjoint(w * lefty, wy * righty, *termsy, f[p], f[p + 1])
            stores += [put(f"y{n}_{p}", r, part) for n, part in parts.items()]
        yield stores

    def rows_adjoint(s, r):
        loads = [(load(f"ey{p}", r), load(f"ty{p}", r)) for p in PARITIES]
        even, odd = ({n: load(f"y{n}_{p}", r) for n in FACE_PARTS if n != "dA"} for p in PARITIES)
        yield
        after = {n: shift_lanes(even[n], -1) for n in ("g2", "h", "bq", "p1", "f1")}
        beyond = {n: shift_lanes(odd[n], -1) for n in ("p1", "f1")}
        stores = []
        for p, (first, second, third) in enumerate(((even, odd, after), (odd, after, beyond))):
            lower, upper = smoothness_adjoint(
                *loads[p], third["p1"], second["g2"], first["p3"], third["f1"], second["h"], first["f2"]
            )
            stores += [put(f"Ry{p}", r, lower + (first["br"] + second["bq"])), put(f"Qy{p}", r, upper)]
        yield stores

    def columns_adjoint(s, r):
        loads = []
        for p in PARITIES:
            loads.append((
                load(f"ex{p}", r), load(f"tx{p}", r),
                load(f"xp1_{p}", r, 2), load(f"xg2_{p}", r, 1), load(f"xp3_{p}", r),
                load(f"xf1_{p}", r, 2), load(f"xh_{p}", r, 1), load(f"xf2_{p}", r),
                load(f"xbr_{p}", r), load(f"xbq_{p}", r, 2),
            ))
        yield
        stores = []
        for p in PARITIES:
            lower, upper = smoothness_adjoint(*loads[p][:8])
            stores += [put(f"Rx{p}", r, lower + loads[p][8]), put(f"Tx{p}", r, upper + loads[p][9])]
        yield stores

    def second_adjoint(s, r):
        columns = [(load(f"Rx{p}", r), load(f"Tx{p}", r, -1)) for p in PARITIES]
        lower = [load(f"Ry{p}", r) for p in PARITIES]
        upper = [load(f"Qy{p}", r) for p in PARITIES]
        yield
        stores = [put(f"Dx{p}", r, columns[p][0] + columns[p][1]) for p in PARITIES]
        stores += [put("Dy0", r, lower[0] + shift_lanes(upper[1], 1)), put("Dy1", r, lower[1] + upper[0])]
        yield stores

    def retreat(s, r):
        early = (1 - s % 2).astype(jnp.float32)
        scale = 1.0 - 0.5 * early
        loads = []
        for p in PARITIES:
            loads.append((
                [load(f"Dx{p}", r, o) for o in (-1, 0, 1)],
                load(f"Dy{p}", r),
                load(f"xdA_{p}", r), load(f"xdA_{p}", r, 1),
                load(f"ydA_{p}", r),
                g[p, rows(r), :],
                held[p, rows(r), :],
            ))
        yield
        stores = []
        d0, d1 = loads[0][1], loads[1][1]
        a0, a1 = loads[0][4], loads[1][4]
        rows_of = (
            ((shift_lanes(d1, 1), d0, d1), a0, a1),
            ((d0, d1, shift_lanes(d0, -1)), a1, shift_lanes(a0, -1)),
        )
        for p in PARITIES:
            dx, _, ax0, ax1, _, old, kept = loads[p]
            dy, ay0, ay1 = rows_of[p]
            back = 6.0 * ((ax0 - ax1) + (ay0 - ay1))
            back = back + ((dx[0] - dx[1]) + (dx[2] - dx[1]))
            back = back + ((dy[0] - dy[1]) + (dy[2] - dy[1]))
            stores += [(g, at(r, p), scale * ((old - back) + early * kept)), (held, at(r, p), old)]
        yield stores

    def backward_step(_, state):
        lag = [(s, pl.multiple_of(r, 8)) for s, r in state]
        together(
            rows_adjoint(*lag[3]),
            weigh(*lag[0]),
            columns_adjoint(*lag[4]),
            differ_rows(*lag[1]),
            face_adjoints(*lag[2]),
            retreat(*lag[7]),
            second_adjoint(*lag[5]),
        )
        return (backward_next(*state[0]),) + state[:7]

    final = STAGES - 1
    lax.fori_loop(
        0,
        count(backward_range, BACKWARD_BLOCK) + 7,
        backward_step,
        (at_rest(final, backward_range(final)[0]),) + (at_rest(final, IDLE),) * 7,
    )

    for n in range(3):
        for p in PARITIES:
            if n == 0:
                value = U[STAGES, p, own, :]
            elif n == 1:
                value = (-DT / 6.0) * rga[p, own, :]
            else:
                value = 2.0 * g[p, own, :]
            stage_out[pl.ds(p, 128, stride=2), :] = value.T
        for device in range(16):
            out[device, n] = stage_out[16 * device : 16 * device + 16, :]


def sweep(core, from_left, from_right):
    full = (2, ROWS, 128)
    f32 = jnp.float32
    plain = pltpu.VMEM(full, f32)
    return pl.pallas_call(
        kernel,
        out_shape=pltpu.VMEM((16, 3, 16, 128), f32),
        in_specs=[pl.BlockSpec(memory_space=pltpu.VMEM)] * 3,
        out_specs=pl.BlockSpec(memory_space=pltpu.VMEM),
        scratch_shapes=[pltpu.VMEM((STAGES + 1,) + full, f32)]
        + [pltpu.VMEM((STAGES, n, ROWS, 128), f32) for n in (6, 3, 3, 8, 2)]
        + [plain] * 4
        + [
            pltpu.VMEM((256, 128), f32),
        ]
        + [pltpu.VMEM((len(group), ROWS, 128), f32) for group in BACKWARD_WORK],
        compiler_params=pltpu.CompilerParams(vmem_limit_bytes=61 * 2**20),
    )(core, from_left, from_right)


def turn_kernel(blocks, core, low, high, rows_ref):
    for n in range(3):
        for device in range(16):
            rows_ref[16 * device : 16 * device + 16, :] = blocks[device, n]
        for p in PARITIES:
            core[n, p] = rows_ref[pl.ds(p, 128, stride=2), :].T
    for p in PARITIES:
        for n, (width, start) in enumerate(((HALO, 0), (HALO, HALO), (HALO_COT, 2 * HALO))):
            low[p, start : start + width, :] = core[n, p, 0:width, :]
            high[p, start : start + width, :] = core[n, p, WIDTH - width : WIDTH, :]


def turn(blocks):
    f32 = jnp.float32
    edge = pltpu.VMEM((2, 2 * HALO + HALO_COT, 128), f32)
    return pl.pallas_call(
        turn_kernel,
        out_shape=(pltpu.VMEM((3, 2, 128, 128), f32), edge, edge),
        in_specs=[pl.BlockSpec(memory_space=pltpu.VMEM)],
        out_specs=[pl.BlockSpec(memory_space=pltpu.VMEM)] * 3,
        scratch_shapes=[pltpu.VMEM((256, 128), f32)],
    )(blocks)


CHAIN = (0, 1, 5, 4, 8, 9, 13, 12, 14, 15, 11, 10, 6, 7, 3, 2)


def columns_held(device):
    place = CHAIN.index(device)
    backwards = lax.axis_index("gx") % 2
    strip = place + backwards * (len(CHAIN) - 1 - 2 * place)
    return pl.ds(pl.multiple_of(strip * WIDTH, WIDTH), WIDTH)


def pack_kernel(level_set, spread_rate, cotangent, blocks, done):
    copies = []
    for device in range(len(CHAIN)):
        columns = columns_held(device)
        for n, ref in enumerate((level_set, spread_rate, cotangent)):
            copies.append(pltpu.make_async_copy(ref.at[:, columns], blocks.at[device, n], done.at[device, n]))
            copies[-1].start()
    for copy in copies:
        copy.wait()


def unpack_kernel(blocks, final_state, rate_gradient, initial_gradient):
    for device in range(len(CHAIN)):
        columns = columns_held(device)
        for n, ref in enumerate((final_state, rate_gradient, initial_gradient)):
            ref[:, columns] = blocks[device, n]


def near(array):
    return pltpu.with_memory_space_constraint(array, pltpu.VMEM)


def shards(level_set, spread_rate, cotangent):
    bands, runs = lax.axis_size("gy"), lax.axis_size("gx")
    vmem = pl.BlockSpec(memory_space=pltpu.VMEM)
    block = jax.ShapeDtypeStruct(level_set.shape, jnp.float32)
    blocks = pl.pallas_call(
        pack_kernel,
        out_shape=pltpu.VMEM((bands, 3, level_set.shape[0], WIDTH), jnp.float32),
        in_specs=[pl.BlockSpec(memory_space=pl.ANY)] * 3,
        out_specs=vmem,
        scratch_shapes=[pltpu.SemaphoreType.DMA((len(CHAIN), 3))],
    )(*(pltpu.with_memory_space_constraint(x, pltpu.HBM) for x in (level_set, spread_rate, cotangent)))
    blocks = near(lax.all_to_all(blocks, "gy", 0, 0))
    core, low, high = turn(blocks)
    place = [k * runs + x for x in range(runs) for k in (CHAIN if x % 2 == 0 else CHAIN[::-1])]
    up = list(zip(place, place[1:] + place[:1]))
    from_left = lax.ppermute(high, ("gy", "gx"), up)
    from_right = lax.ppermute(low, ("gy", "gx"), [(b, a) for a, b in up])
    core, from_left, from_right = near(core), near(from_left), near(from_right)
    done = near(lax.all_to_all(sweep(core, from_left, from_right), "gy", 0, 0))
    return pl.pallas_call(
        unpack_kernel,
        out_shape=(block,) * 3,
        in_specs=[vmem],
        out_specs=(vmem,) * 3,
    )(done)


def solution(mesh):
    spec = P("gy", "gx")
    return jax.shard_map(
        shards, mesh=mesh, in_specs=(spec,) * 3, out_specs=(spec,) * 3, check_vma=False
    )
```
